512 devices in a mesh: dp: 16 (over y_lo, x, core), expert: 32 (over y_hi, z).
Axes of the slice: x: 4, y: 8 (y_hi: 4, y_lo: 2; y = y_hi * 2 + y_lo), z: 8, core: 2. Of those that a mesh axis runs over, the one named last changes fastest.
Arguments:
- events: bfloat16 [1024, 1024], P(('dp', 'expert')), may hold values from -6 to 6
- labels: int32 [1024, 4], P(('dp', 'expert')), may hold values 0 or 1
- w_in: bfloat16 [32, 1024, 4096], P('expert', None, 'dp'), may hold values from -0.1875 to 0.1875
- w_out: bfloat16 [32, 4096, 1024], P('expert', 'dp'), may hold values from -0.09375 to 0.09375
- gate_weight: bfloat16 [4, 1024, 32], replicated, may hold values from -4 to 4
- tower_in: bfloat16 [4, 1024, 256], replicated, may hold values from -0.1875 to 0.1875
- tower_bias: float32 [4, 256], replicated, may hold values from -3 to 3
- tower_out: float32 [4, 256], replicated, may hold values from -0.75 to 0.75
- tower_out_bias: float32 [4], replicated, may hold values from -3 to 3
Outputs:
- grad_in: bfloat16 [32, 1024, 4096], P('expert', None, 'dp')
- grad_out: bfloat16 [32, 4096, 1024], P('expert', 'dp')
- grad_gate: float32 [4, 1024, 32], P(None, None, 'expert')
The draws below stay inside these ranges and needn't reach their ends.
All inputs are finite; a program needn't handle non-finite values. No bound on the sum of `labels` on one device may be relied on, other than what follows from the above.
Results may differ from the reference program's by a relative error of at most 0.035.
Values may be sent and summed in bfloat16 or wider, within the bound.
A program may use at most 64 MiB of HBM per device.

```python
import jax
import jax.numpy as jnp
from jax import lax

D = 1024
H = 4096
TASKS = 4
TW = 256
E = 32
ROWS = 1024
N_DP = 16


def draw_gate_weight(key, part):
    key = jax.random.fold_in(key, 5)
    first = jax.random.fold_in(key, 0)
    values = jax.random.normal(first, (TASKS, D, E), jnp.float32) * (2.0 / D ** 0.5)
    return jnp.clip(values, -4.0, 4.0).astype(jnp.bfloat16)


def set_ends(values, rng, smallest, high):
    longest = values.shape.index(max(values.shape))
    spots = []
    for shift in (0, 1):
        where = [jax.random.randint(jax.random.fold_in(rng, axis), (), 0, length) for axis, length in enumerate(values.shape)]
        where[longest] = (where[longest] + shift) % values.shape[longest]
        spots.append(tuple(where))
    return values.at[spots[0]].set(smallest).at[spots[1]].set(high)


def shard_levels(rng, dims, shards, least, top_value):
    level = 1.0
    for axis_at, shards_of in shards:
        heights = jax.random.uniform(jax.random.fold_in(jax.random.fold_in(rng, 6), axis_at), (shards_of,), jnp.float32, least / len(shards), top_value / len(shards))
        level = level * jnp.repeat(jnp.exp(heights), dims[axis_at] // shards_of).reshape((-1,) + (1,) * (len(dims) - 1 - axis_at))
    return level


def normal_values(key, dims, scale, reach, cuts=(), held_as=jnp.bfloat16):
    array = scale * jax.random.normal(key, dims, jnp.float32)
    if cuts:
        array = array * shard_levels(key, dims, cuts, -0.22, 0.18)
    return jnp.clip(array, -reach, reach).astype(held_as)


def setup_inputs(seed: int = 0) -> dict:
    seeds = jax.random.split(jax.random.key(seed), 10)
    return {
        "events": normal_values(seeds[0], (ROWS, D), 1.0, 6.0, ((0, 512),)),
        "labels": set_ends((jax.random.randint(seeds[1], (ROWS, TASKS), 0, 2) < 1).astype(jnp.int32), jax.random.fold_in(seeds[1], 1), 0, 1),
        "w_in": normal_values(seeds[2], (E, D, H), D ** -0.5, 0.1875, ((0, 32), (2, 16))),
        "w_out": normal_values(seeds[3], (E, H, D), H ** -0.5, 0.09375, ((0, 32), (1, 16))),
        "gate_weight": draw_gate_weight(jax.random.fold_in(seeds[9], 71), 0),
        "tower_in": normal_values(seeds[5], (TASKS, D, TW), D ** -0.5, 0.1875),
        "tower_bias": normal_values(seeds[6], (TASKS, TW), 0.5, 3.0, (), jnp.float32),
        "tower_out": normal_values(seeds[7], (TASKS, TW), (TW // 4) ** -0.5, 0.75, (), jnp.float32),
        "tower_out_bias": normal_values(seeds[8], (TASKS,), 1.0, 3.0, (), jnp.float32),
    }


def gelu_tanh(value):
    return jax.nn.gelu(value, approximate=True)

def tower_apply(mixed, tower_in, tower_bias, tower_out, tower_out_bias):
    tower_pre = jnp.einsum('trd,tdk->trk', mixed, tower_in.astype(jnp.float32), precision=lax.Precision.HIGHEST) + tower_bias[:, None, :]
    return lax.optimization_barrier(jnp.sum(gelu_tanh(tower_pre) * tower_out[:, None, :], -1)) + tower_out_bias[:, None]

def reference(events, labels, w_in, w_out, gate_weight, tower_in, tower_bias, tower_out, tower_out_bias):
    rows = events.shape[0]
    blocks = N_DP
    width = w_in.shape[2] // blocks

    def forward(pair):
        weight_in, weight_out = pair
        pre = jnp.dot(events, weight_in, preferred_element_type=jnp.float32)
        hidden = gelu_tanh(pre).astype(jnp.bfloat16)
        parts = jnp.einsum('rjk,jkd->jrd', hidden.reshape(rows, blocks, width).astype(jnp.float32), weight_out.reshape(blocks, width, -1).astype(jnp.float32), precision=lax.Precision.HIGHEST)
        rounded = lax.optimization_barrier(parts.astype(jnp.bfloat16)).astype(jnp.float32)
        return lax.optimization_barrier(jnp.sum(rounded, 0)).astype(jnp.bfloat16)
    expert_out = lax.map(forward, (w_in, w_out))
    events_wide = events.astype(jnp.float32)
    gate_logits = jnp.einsum('rd,tde->tre', events_wide, gate_weight.astype(jnp.float32), precision=lax.Precision.HIGHEST)
    probs = jax.nn.softmax(gate_logits, axis=-1)
    outs_wide = expert_out.astype(jnp.float32)
    mixed = jnp.einsum('tre,erd->trd', probs, outs_wide, precision=lax.Precision.HIGHEST).astype(jnp.bfloat16)
    targets = labels.T.astype(jnp.float32)

    def tower_of(value):
        return tower_apply(value, tower_in, tower_bias, tower_out, tower_out_bias)
    logit, tower_back = jax.vjp(tower_of, mixed.astype(jnp.float32))
    dmixed = tower_back(jax.nn.sigmoid(logit) - targets)[0].astype(jnp.bfloat16)
    dmixed_wide = lax.optimization_barrier(dmixed).astype(jnp.float32)
    dprob = jnp.einsum('trd,erd->tre', dmixed_wide, outs_wide, precision=lax.Precision.HIGHEST)
    dgate = probs * (dprob - lax.optimization_barrier(jnp.sum(probs * dprob, -1, keepdims=True)))
    grad_gate = jnp.einsum('rd,tre->tde', events_wide, dgate, precision=lax.Precision.HIGHEST)
    dexpert = jnp.einsum('tre,trd->erd', probs, dmixed_wide, precision=lax.Precision.HIGHEST).astype(jnp.bfloat16)

    def backward(triple):
        weight_in, weight_out, grad_rows = triple
        pre = jnp.dot(events, weight_in, preferred_element_type=jnp.float32)
        hidden = gelu_tanh(pre).astype(jnp.bfloat16)
        dhidden = jnp.dot(grad_rows, weight_out.T, preferred_element_type=jnp.float32)
        gelu_back = jax.vjp(gelu_tanh, pre)[1]
        dpre = gelu_back(dhidden)[0].astype(jnp.bfloat16)
        grad_second = jnp.dot(hidden.T, grad_rows, preferred_element_type=jnp.float32).astype(jnp.bfloat16)
        grad_first = jnp.dot(events.T, dpre, preferred_element_type=jnp.float32).astype(jnp.bfloat16)
        return (grad_first, grad_second)
    grad_in, grad_out = lax.map(backward, (w_in, w_out, dexpert))
    return (grad_in, grad_out, grad_gate)
```

```python
import functools
import math

import jax
import jax.numpy as jnp
from jax import lax
from jax.experimental import pallas as pl
from jax.experimental.pallas import tpu as pltpu
from jax.sharding import PartitionSpec as P

MESH = pl.DeviceIdType.MESH
BF = jnp.bfloat16
F32 = jnp.float32
LANES = 128
CORES = 2
GELU_A = math.sqrt(2.0 / math.pi)
GELU_B = 0.044715


def dot(a, b):
    return jnp.dot(a, b, preferred_element_type=F32)


def dot_nt(a, b):
    return lax.dot_general(a, b, (((1,), (1,)), ((), ())), preferred_element_type=F32)


def dot_tn(a, b):
    return lax.dot_general(a, b, (((0,), (0,)), ((), ())), preferred_element_type=F32)


def split(a):
    high = a.astype(BF)
    return high, (a - high.astype(F32)).astype(BF)


def gelu_parts(x):
    t = jnp.tanh(GELU_A * (x + GELU_B * x * x * x))
    value = 0.5 * x * (1.0 + t)
    slope = 0.5 * (1.0 + t) + 0.5 * x * (1.0 - t * t) * GELU_A * (1.0 + 3.0 * GELU_B * x * x)
    return value, slope


def ones_where(shape, test):
    rows = lax.broadcasted_iota(jnp.int32, shape, 0)
    cols = lax.broadcasted_iota(jnp.int32, shape, 1)
    return jnp.where(test(rows, cols), 1.0, 0.0).astype(BF)


def kernel(
    n_ex,
    n_chip,
    tasks,
    width,
    own_ref,
    labels_ref,
    w_in_hbm,
    w_out_hbm,
    gate_hbm,
    tower_hbm,
    bias_ref,
    out_ref,
    out_bias_ref,
    grad_in_ref,
    grad_out_ref,
    grad_gate_ref,
    first_buf,
    shuf,
    ev_a,
    ev_b,
    w_in_v,
    w_out_v,
    fused,
    tower_v,
    gate_v,
    gate_cat,
    part_own,
    part_send,
    part_recv,
    term_send,
    term_recv,
    small,
    prob_own,
    share_own,
    share,
    slope_v,
    hidden_t,
    ev_t,
    dt_chunk,
    dt_first,
    dt_a,
    dt_b,
    dg_chunk,
    dg_first,
    dg_a,
    dg_b,
    acc_in,
    acc_mid,
    acc_gate,
    load_sem,
    w_send,
    w_recv,
    first_send,
    first_recv,
    ev_send,
    ev_recv,
    evf_send,
    evf_recv,
    part_ssem,
    part_rsem,
    term_ssem,
    term_rsem,
    dt1_send,
    dt1_recv,
    dg1_send,
    dg1_recv,
    dt_send,
    dt_recv,
    dtf_send,
    dtf_recv,
    dg_send,
    dg_recv,
    dgf_send,
    dgf_recv,
):
    dp = lax.axis_index("dp")
    ex = lax.axis_index("expert")
    core = lax.rem(dp, CORES)
    chip = lax.div(dp, CORES)
    sibling = (dp + 1 - 2 * core, ex)
    feat = ev_a.shape[2]
    wide = tasks * width
    blk = ev_a.shape[1]
    hid = w_out_v.shape[0]
    gates = gate_cat.shape[1]
    experts = gates // tasks
    g_rows = ev_t.shape[2]
    per_group = g_rows // blk
    half = n_chip // per_group

    def ex_peer(k):
        return (dp, lax.rem(ex + k, n_ex))

    def chip_peer(k):
        return (lax.rem(chip + k, n_chip) * CORES + core, ex)

    def remote(src, dst, send, recv, to):
        return pltpu.make_async_remote_copy(
            src_ref=src, dst_ref=dst, send_sem=send, recv_sem=recv, device_id=to, device_id_type=MESH
        )

    barrier = pltpu.get_barrier_semaphore()

    @pl.loop(1, n_ex)
    def _(k):
        pl.semaphore_signal(barrier, inc=1, device_id=ex_peer(k), device_id_type=MESH)

    @pl.loop(1, n_chip)
    def _(k):
        pl.semaphore_signal(barrier, inc=1, device_id=chip_peer(k), device_id_type=MESH)

    pl.semaphore_signal(barrier, inc=1, device_id=sibling, device_id_type=MESH)

    loads = [
        pltpu.make_async_copy(src, dst, load_sem.at[i])
        for i, (src, dst) in enumerate(
            (
                (w_out_hbm.at[0], w_out_v),
                (tower_hbm, tower_v),
                (w_in_hbm.at[0], w_in_v.at[0]),
                (gate_hbm, gate_v),
            )
        )
    ]
    for load in loads:
        load.start()
    pl.semaphore_wait(barrier, n_ex + n_chip - 1)

    def spread(src_of, dst, send, recv):
        @pl.loop(1, n_ex)
        def _(k):
            to = ex_peer(k)
            remote(src_of(to[1]), dst.at[ex], send, recv, to).start()

    def spread_wait(dst, send, recv):
        every = dst.at[pl.ds(0, n_ex - 1)]
        copy = remote(every, every, send, recv, ex_peer(1))
        copy.wait_recv()
        copy.wait_send()

    def unshuffle(src, dst, count):
        rows = src.shape[1]
        shuf[pl.ds(0, n_ex * rows), :] = src[...].astype(F32).reshape(n_ex * rows, LANES)
        for j in range(count):
            for i in range(2):
                piece = shuf[pl.ds(j * 2 + i, n_ex, stride=rows), :]
                dst[i * n_ex : (i + 1) * n_ex, j * LANES : (j + 1) * LANES] = piece.astype(BF)

    spread(lambda _: own_ref, first_buf, first_send, first_recv)
    first_buf[ex] = own_ref[...]
    w_in_copy = remote(w_in_hbm.at[0], w_in_v.at[1], w_send.at[0], w_recv.at[0], sibling)
    w_in_copy.start()
    for t in range(tasks):
        for j in range(width // LANES):
            for i in range(2):
                at = (t * (width // LANES) + j) * 2 + i
                cols = slice(j * LANES, (j + 1) * LANES)
                small[0, at : at + 1, :] = bias_ref[t : t + 1, cols]
                small[1, at : at + 1, :] = out_ref[t : t + 1, cols]
    loads[0].wait()
    loads[1].wait()
    for t in range(tasks):
        cols = slice(t * width, (t + 1) * width)
        fused[0, :, cols] = dot(w_out_v[...], tower_v[t]).astype(BF)
    fused_copy = remote(fused.at[0], fused.at[1], w_send.at[1], w_recv.at[1], sibling)
    fused_copy.start()
    loads[3].wait()
    gate_cat[...] = jnp.concatenate([gate_v[t].astype(F32) for t in range(tasks)], axis=1).astype(BF)
    same_task = ones_where((gates, gates), lambda r, c: r // experts == c // experts)
    own_share = ones_where(
        (gates, wide), lambda r, c: (r // experts == c // width) & (r % experts == ex)
    )

    def gate_probs(rows):
        logits = dot(rows, gate_cat[...])
        lane = lax.broadcasted_iota(jnp.int32, logits.shape, 1) // experts
        top = jnp.zeros_like(logits)
        for t in range(tasks):
            mine = lane == t
            peak = jnp.max(jnp.where(mine, logits, -jnp.inf), axis=1, keepdims=True)
            top = jnp.where(mine, peak, top)
        grown = jnp.exp(logits - top)
        high, low = split(grown)
        return grown / (dot(high, same_task) + dot(low, same_task))

    def shares(probs):
        high, low = split(probs)
        return dot(high, own_share) + dot(low, own_share)

    spread_wait(first_buf, first_send, first_recv)
    unshuffle(first_buf, ev_a.at[chip], feat // LANES)

    def to_chips(buf, send, recv):
        @pl.loop(1, n_chip)
        def _(k):
            mine = buf.at[chip]
            remote(mine, buf.at[chip], send.at[k], recv.at[chip], chip_peer(k)).start()

    def arrived(buf, send, recv, slot):
        remote(buf.at[slot], buf.at[slot], send.at[0], recv.at[slot], sibling).wait_recv()

    def forward(buf, other, send, recv, slot):
        remote(buf.at[slot], other.at[slot], send.at[slot], recv.at[slot], sibling).start()

    def sends_done(buf, send, first, last):
        @pl.loop(first, last)
        def _(k):
            remote(buf.at[0], buf.at[0], send.at[k], send.at[k], sibling).wait_send()

    to_chips(ev_a, ev_send, ev_recv)
    forward(ev_a, ev_b, evf_send, evf_recv, chip)
    probs = gate_probs(ev_a[chip])
    prob_own[...] = probs
    share_own[...] = shares(probs)
    loads[2].wait()
    w_in_copy.wait_recv()
    fused_copy.wait_recv()

    def forward_block(slot):
        rows = ev_a[slot]
        part = None
        for h in range(2):
            pre = dot(rows, w_in_v[h])
            hidden = gelu_parts(pre)[0].astype(BF)
            term = dot(hidden, fused[h])
            part = term if part is None else part + term
        return part

    part_own[...] = forward_block(chip)

    @pl.loop(1, n_chip)
    def _(k):
        slot = lax.rem(chip + k, n_chip)
        arrived(ev_a, ev_send, ev_recv, slot)
        forward(ev_a, ev_b, evf_send, evf_recv, slot)
        part_send[slot] = forward_block(slot).astype(BF)
        remote(
            part_send.at[slot], part_recv.at[chip], part_ssem.at[k], part_rsem.at[chip], chip_peer(k)
        ).start()

    def prepare(group, buf, at):
        rows = buf[pl.ds(at * per_group, per_group)].reshape(g_rows, feat)
        pre = dot(rows, w_in_v[0])
        value, slope = gelu_parts(pre)
        slope_v[group] = slope
        hidden_t[group] = value.T.astype(BF)
        ev_t[group] = rows.astype(F32).T.astype(BF)
        share[group] = shares(gate_probs(rows))

    @pl.loop(0, half)
    def _(g):
        prepare(g, ev_a, g)

    @pl.loop(0, n_chip)
    def _(k):
        arrived(ev_b, evf_send, evf_recv, k)

    @pl.loop(0, half)
    def _(g):
        prepare(half + g, ev_b, g)

    total = part_own[...]
    for k in range(1, n_chip):
        slot = lax.rem(chip + k, n_chip)
        arrived(part_recv, part_ssem, part_rsem, slot)
        total = total + part_recv[slot].astype(F32)
    terms = total * share_own[...]
    crow = term_send.shape[1]
    for j in range(wide // LANES):
        for i in range(2):
            shuf[pl.ds(j * 2 + i, n_ex, stride=crow), :] = terms[
                i * n_ex : (i + 1) * n_ex, j * LANES : (j + 1) * LANES
            ]
    term_send[...] = shuf[pl.ds(0, n_ex * crow), :].reshape(n_ex, crow, LANES).astype(BF)
    spread(lambda to: term_send.at[to], term_recv, term_ssem, term_rsem)
    term_recv[ex] = term_send[ex]
    spread_wait(term_recv, term_ssem, term_rsem)

    def both_halves(value):
        row = lax.broadcasted_iota(jnp.int32, value.shape, 0)
        step = 2
        while step < 2 * (width // LANES):
            up = pltpu.roll(value, crow - step, 0)
            down = pltpu.roll(value, step, 0)
            value = value + jnp.where((row // step) % 2 == 0, up, down)
            step *= 2
        return value

    mixed = jnp.sum(term_recv[...].astype(F32), axis=0)
    act, act_slope = gelu_parts(mixed + small[0])
    weight = small[1]
    summed = jnp.broadcast_to(jnp.sum(act * weight, axis=1, keepdims=True), mixed.shape)
    row = lax.broadcasted_iota(jnp.int32, mixed.shape, 0)
    task_of = row // (2 * (width // LANES))
    logit = both_halves(summed)
    target = jnp.zeros_like(logit)
    for t in range(tasks):
        logit = logit + jnp.where(task_of == t, out_bias_ref[t], 0.0)
        for i in range(2):
            label = labels_ref[i, t].astype(F32)
            target = target + jnp.where((task_of == t) & (row % 2 == i), label, 0.0)
    dlogit = 1.0 / (1.0 + jnp.exp(-logit)) - target
    dt = (dlogit * weight * act_slope).astype(BF)
    dt_chunk[...] = dt
    spread(lambda _: dt_chunk, dt_first, dt1_send, dt1_recv)
    dt_first[ex] = dt

    prod = (term_recv[...].astype(F32) * dt.astype(F32)[None]).reshape(n_ex * crow, LANES)
    high, low = split(prod)
    all_ones = jnp.ones((LANES, gates), BF)
    sums = dot(high, all_ones) + dot(low, all_ones)
    at = lax.broadcasted_iota(jnp.int32, sums.shape, 0)
    lane = lax.broadcasted_iota(jnp.int32, sums.shape, 1)
    here = lane == (at % crow) // (2 * (width // LANES)) * experts + at // crow
    sums = jnp.where(here, sums, 0.0)
    pick = ones_where((16, n_ex * crow), lambda r, c: (r == c % 2))
    high, low = split(sums)
    moved = dot(pick, high) + dot(pick, low)
    high, low = split(moved)
    weighted = dot(high, same_task) + dot(low, same_task)
    own_rows = jnp.concatenate(
        [
            prob_own[pl.ds(ex, 1), :],
            prob_own[pl.ds(n_ex + ex, 1), :],
            jnp.zeros((14, gates), F32),
        ],
        axis=0,
    )
    dg = (moved - own_rows * weighted).astype(BF)
    dg_chunk[...] = dg
    spread(lambda _: dg_chunk, dg_first, dg1_send, dg1_recv)
    dg_first[ex] = dg

    spread_wait(dt_first, dt1_send, dt1_recv)
    unshuffle(dt_first, dt_a.at[chip], wide // LANES)
    to_chips(dt_a, dt_send, dt_recv)
    forward(dt_a, dt_b, dtf_send, dtf_recv, chip)
    spread_wait(dg_first, dg1_send, dg1_recv)
    rows16 = dg_first.shape[1]
    shuf2 = shuf.at[pl.ds(0, n_ex * rows16)]
    shuf2[:, 0:gates] = dg_first[...].astype(F32).reshape(n_ex * rows16, gates)
    for i in range(2):
        dg_a[chip, i * n_ex : (i + 1) * n_ex, :] = shuf2[pl.ds(i, n_ex, stride=rows16), :][
            :, 0:gates
        ].astype(BF)
    to_chips(dg_a, dg_send, dg_recv)
    forward(dg_a, dg_b, dgf_send, dgf_recv, chip)

    @pl.loop(1, n_chip)
    def _(k):
        slot = lax.rem(chip + k, n_chip)
        arrived(dt_a, dt_send, dt_recv, slot)
        forward(dt_a, dt_b, dtf_send, dtf_recv, slot)
        arrived(dg_a, dg_send, dg_recv, slot)
        forward(dg_a, dg_b, dgf_send, dgf_recv, slot)

    acc_in[...] = jnp.zeros_like(acc_in)
    acc_mid[...] = jnp.zeros_like(acc_mid)
    acc_gate[...] = jnp.zeros_like(acc_gate)

    def backward(group, ev_buf, dt_buf, dg_buf, at):
        span = pl.ds(at * per_group, per_group)
        dout = (dt_buf[span].reshape(g_rows, wide).astype(F32) * share[group]).astype(BF)
        dhidden = dot_nt(dout, fused[0])
        dpre = (dhidden * slope_v[group]).astype(BF)
        acc_in[...] += dot(ev_t[group], dpre)
        acc_mid[...] += dot(hidden_t[group], dout)
        rows = ev_buf[span].reshape(g_rows, feat)
        acc_gate[...] += dot(dg_buf[span].reshape(g_rows, gates).astype(F32).T.astype(BF), rows)

    @pl.loop(0, half)
    def _(g):
        backward(g, ev_a, dt_a, dg_a, g)

    @pl.loop(0, n_chip)
    def _(k):
        arrived(dt_b, dtf_send, dtf_recv, k)
        arrived(dg_b, dgf_send, dgf_recv, k)

    @pl.loop(0, half)
    def _(g):
        backward(half + g, ev_b, dt_b, dg_b, g)

    grad_in_ref[...] = acc_in[...].astype(BF)
    mid = acc_mid[...].astype(BF)
    result = None
    for t in range(tasks):
        term = dot_nt(mid[:, t * width : (t + 1) * width], tower_v[t])
        result = term if result is None else result + term
    grad_out_ref[...] = result.astype(BF)
    mine = ones_where((grad_gate_ref.shape[0], gates), lambda r, c: (c == r * experts + ex))
    high, low = split(acc_gate[...])
    grad_gate_ref[...] = dot(mine, high) + dot(mine, low)

    w_in_copy.wait_send()
    fused_copy.wait_send()
    for buf, send in (
        (ev_a, ev_send),
        (part_send, part_ssem),
        (dt_a, dt_send),
        (dg_a, dg_send),
    ):
        sends_done(buf, send, 1, n_chip)
    for buf, send in ((ev_a, evf_send), (dt_a, dtf_send), (dg_a, dgf_send)):
        sends_done(buf, send, 0, n_chip)


def per_device(
    n_dp,
    n_ex,
    events,
    labels,
    w_in,
    w_out,
    gate_weight,
    tower_in,
    tower_bias,
    tower_out,
    tower_out_bias,
):
    tasks, feat, width = tower_in.shape
    experts = gate_weight.shape[2]
    hid = w_out.shape[1]
    n_chip = n_dp // CORES
    own = events.shape[0]
    blk = own * n_ex
    plane = n_chip * blk
    g_rows = max(plane // 2, blk)
    groups = 2 * plane // g_rows
    wide = tasks * width
    gates = tasks * experts
    chunk = own * feat // LANES
    chunk_t = own * wide // LANES
    chunk_events = events.reshape(own, feat // LANES, LANES).transpose(1, 0, 2).reshape(chunk, LANES)
    vmem = pl.BlockSpec(memory_space=pltpu.VMEM)
    smem = pl.BlockSpec(memory_space=pltpu.SMEM)
    hbm = pl.BlockSpec(memory_space=pl.ANY)
    dma = pltpu.SemaphoreType.DMA
    scratch = [
        pltpu.VMEM((n_ex, chunk, LANES), BF),
        pltpu.VMEM((n_ex * max(chunk, chunk_t, 16), LANES), F32),
        pltpu.VMEM((n_chip, blk, feat), BF),
        pltpu.VMEM((n_chip, blk, feat), BF),
        pltpu.VMEM((2, feat, hid), BF),
        pltpu.VMEM((hid, feat), BF),
        pltpu.VMEM((2, hid, wide), BF),
        pltpu.VMEM((tasks, feat, width), BF),
        pltpu.VMEM((tasks, feat, experts), BF),
        pltpu.VMEM((feat, gates), BF),
        pltpu.VMEM((blk, wide), F32),
        pltpu.VMEM((n_chip, blk, wide), BF),
        pltpu.VMEM((n_chip, blk, wide), BF),
        pltpu.VMEM((n_ex, chunk_t, LANES), BF),
        pltpu.VMEM((n_ex, chunk_t, LANES), BF),
        pltpu.VMEM((2, chunk_t, LANES), F32),
        pltpu.VMEM((blk, gates), F32),
        pltpu.VMEM((blk, wide), F32),
        pltpu.VMEM((groups, g_rows, wide), F32),
        pltpu.VMEM((groups, g_rows, hid), F32),
        pltpu.VMEM((groups, hid, g_rows), BF),
        pltpu.VMEM((groups, feat, g_rows), BF),
        pltpu.VMEM((chunk_t, LANES), BF),
        pltpu.VMEM((n_ex, chunk_t, LANES), BF),
        pltpu.VMEM((n_chip, blk, wide), BF),
        pltpu.VMEM((n_chip, blk, wide), BF),
        pltpu.VMEM((16, gates), BF),
        pltpu.VMEM((n_ex, 16, gates), BF),
        pltpu.VMEM((n_chip, blk, gates), BF),
        pltpu.VMEM((n_chip, blk, gates), BF),
        pltpu.VMEM((feat, hid), F32),
        pltpu.VMEM((hid, wide), F32),
        pltpu.VMEM((gates, feat), F32),
        dma((4,)),
        dma((2,)),
        dma((2,)),
        dma,
        dma,
        dma((n_chip,)),
        dma((n_chip,)),
        dma((n_chip,)),
        dma((n_chip,)),
        dma((n_chip,)),
        dma((n_chip,)),
        dma,
        dma,
        dma,
        dma,
        dma,
        dma,
    ] + [dma((n_chip,))] * 8
    grad_in, grad_out, grad_gate = pl.pallas_call(
        functools.partial(kernel, n_ex, n_chip, tasks, width),
        out_shape=(
            jax.ShapeDtypeStruct((feat, hid), BF),
            jax.ShapeDtypeStruct((hid, feat), BF),
            jax.ShapeDtypeStruct((8, feat), F32),
        ),
        in_specs=[vmem, smem, hbm, hbm, hbm, hbm, vmem, vmem, smem],
        out_specs=(vmem, vmem, vmem),
        scratch_shapes=scratch,
        compiler_params=pltpu.CompilerParams(
            collective_id=0, has_side_effects=True, vmem_limit_bytes=48 * 1024 * 1024
        ),
    )(
        chunk_events,
        labels,
        w_in,
        w_out,
        gate_weight,
        tower_in,
        tower_bias,
        tower_out,
        tower_out_bias,
    )
    return grad_in[None], grad_out[None], grad_gate[:tasks, :, None]


def solution(mesh):
    placed = (
        P(("dp", "expert"), None),
        P(("dp", "expert"), None),
        P("expert", None, "dp"),
        P("expert", "dp", None),
        P(),
        P(),
        P(),
        P(),
        P(),
    )
    return jax.shard_map(
        functools.partial(per_device, mesh.shape["dp"], mesh.shape["expert"]),
        mesh=mesh,
        in_specs=placed,
        out_specs=(P("expert", None, "dp"), P("expert", "dp", None), P(None, None, "expert")),
        check_vma=False,
    )
```

```python
import functools
import math

import jax
import jax.numpy as jnp
from jax import lax
from jax.experimental import pallas as pl
from jax.experimental.pallas import tpu as pltpu
from jax.sharding import PartitionSpec as P

MESH = pl.DeviceIdType.MESH
BF = jnp.bfloat16
F32 = jnp.float32
LANES = 128
CORES = 2
GELU_A = math.sqrt(2.0 / math.pi)
GELU_B = 0.044715
VMEM_MIB = 34


def dot(a, b):
    return jnp.dot(a, b, preferred_element_type=F32)


def dot_nt(a, b):
    return lax.dot_general(a, b, (((1,), (1,)), ((), ())), preferred_element_type=F32)


def dot_tn(a, b):
    return lax.dot_general(a, b, (((0,), (0,)), ((), ())), preferred_element_type=F32)


def split(a):
    high = a.astype(BF)
    return high, (a - high.astype(F32)).astype(BF)


def gelu_parts(x):
    t = jnp.tanh(GELU_A * (x + GELU_B * x * x * x))
    value = 0.5 * x * (1.0 + t)
    slope = 0.5 * (1.0 + t) + 0.5 * x * (1.0 - t * t) * GELU_A * (1.0 + 3.0 * GELU_B * x * x)
    return value, slope


def ones_where(shape, test):
    rows = lax.broadcasted_iota(jnp.int32, shape, 0)
    cols = lax.broadcasted_iota(jnp.int32, shape, 1)
    return jnp.where(test(rows, cols), 1.0, 0.0).astype(BF)


def kernel(
    n_ex,
    n_chip,
    tasks,
    width,
    own_hbm,
    labels_hbm,
    w_in_hbm,
    w_out_hbm,
    gate_hbm,
    tower_hbm,
    bias_hbm,
    out_hbm,
    out_bias_hbm,
    grad_in_ref,
    grad_out_ref,
    grad_gate_ref,
    first_buf,
    shuf,
    ev_a,
    ev_b,
    w_in_v,
    w_out_v,
    fused,
    tower_v,
    gate_v,
    labels_v,
    bias_v,
    out_v,
    out_bias_v,
    part_own,
    part_send,
    part_recv,
    term_send,
    term_recv,
    small,
    prob_own,
    share_own,
    share,
    slope_v,
    hidden_t,
    ev_t,
    dt_chunk,
    dt_first,
    dt_a,
    dt_b,
    dg_chunk,
    dg_first,
    dg_a,
    dg_b,
    acc_in,
    acc_mid,
    acc_gate,
    load_sem,
    w_send,
    w_recv,
    first_send,
    first_recv,
    ev_send,
    ev_recv,
    evf_send,
    evf_recv,
    part_ssem,
    part_rsem,
    term_ssem,
    term_rsem,
    dt1_send,
    dt1_recv,
    dg1_send,
    dg1_recv,
    dt_send,
    dt_recv,
    dtf_send,
    dtf_recv,
    dg_send,
    dg_recv,
    dgf_send,
    dgf_recv,
):
    dp = lax.axis_index("dp")
    ex = lax.axis_index("expert")
    core = lax.rem(dp, CORES)
    chip = lax.div(dp, CORES)
    n_x = n_chip // 2
    n_yh = min(4, n_ex)
    n_z = n_ex // n_yh
    x, y_lo = lax.rem(chip, n_x), lax.div(chip, n_x)
    y = lax.div(ex, n_z) * 2 + y_lo
    sibling = (dp + 1 - 2 * core, ex)
    feat = ev_a.shape[2]
    wide = tasks * width
    blk = ev_a.shape[1]
    hid = w_out_v.shape[0]
    gates = gate_v.shape[0]
    experts = gates // tasks
    g_rows = ev_t.shape[2]
    per_group = g_rows // blk
    half = n_chip // per_group

    def ex_peer(k):
        return (dp, lax.rem(ex + k, n_ex))

    def chip_peer(k):
        return (lax.rem(chip + k, n_chip) * CORES + core, ex)

    def x_peer(step):
        return ((y_lo * n_x + lax.rem(x + step + n_x, n_x)) * CORES + core, ex)

    def y_peer(step):
        to = lax.rem(y + step + 2 * n_yh, 2 * n_yh)
        return (
            (lax.rem(to, 2) * n_x + x) * CORES + core,
            lax.div(to, 2) * n_z + lax.rem(ex, n_z),
        )

    def remote(src, dst, send, recv, to):
        return pltpu.make_async_remote_copy(
            src_ref=src, dst_ref=dst, send_sem=send, recv_sem=recv, device_id=to, device_id_type=MESH
        )

    barrier = pltpu.get_barrier_semaphore()

    @pl.loop(1, n_ex)
    def _(k):
        pl.semaphore_signal(barrier, inc=1, device_id=ex_peer(k), device_id_type=MESH)

    @pl.loop(1, n_chip)
    def _(k):
        pl.semaphore_signal(barrier, inc=1, device_id=chip_peer(k), device_id_type=MESH)

    pl.semaphore_signal(barrier, inc=1, device_id=sibling, device_id_type=MESH)
    pl.semaphore_signal(barrier, inc=1, device_id=y_peer(2 * y_lo - 1), device_id_type=MESH)

    loads = [
        pltpu.make_async_copy(src, dst, load_sem.at[i])
        for i, (src, dst) in enumerate(
            (
                (w_out_hbm.at[0], w_out_v),
                (tower_hbm, tower_v),
                (w_in_hbm.at[0], w_in_v.at[0]),
                (gate_hbm, gate_v),
                (labels_hbm, labels_v),
                (bias_hbm, bias_v),
                (out_hbm, out_v),
                (out_bias_hbm, out_bias_v),
                (own_hbm, first_buf.at[ex]),
            )
        )
    ]
    for load in loads:
        load.start()
    pl.semaphore_wait(barrier, n_ex + n_chip)

    def spread(src_of, dst, send, recv):
        @pl.loop(1, n_ex)
        def _(k):
            to = ex_peer(k)
            remote(src_of(to[1]), dst.at[ex], send, recv, to).start()

    def spread_wait(dst, send, recv):
        every = dst.at[pl.ds(0, n_ex - 1)]
        copy = remote(every, every, send, recv, ex_peer(1))
        copy.wait_recv()
        copy.wait_send()

    def unshuffle(src, dst, count):
        rows = src.shape[1]
        shuf[pl.ds(0, n_ex * rows), :] = src[...].astype(F32).reshape(n_ex * rows, LANES)
        for j in range(count):
            for i in range(2):
                piece = shuf[pl.ds(j * 2 + i, n_ex, stride=rows), :]
                dst[i * n_ex : (i + 1) * n_ex, j * LANES : (j + 1) * LANES] = piece.astype(BF)

    spread(lambda _: own_hbm, first_buf, first_send, first_recv)
    w_in_copy = remote(w_in_hbm.at[0], w_in_v.at[1], w_send.at[0], w_recv.at[0], sibling)
    w_in_copy.start()
    for load in loads[4:9]:
        load.wait()
    for t in range(tasks):
        for j in range(width // LANES):
            at = (t * (width // LANES) + j) * 2
            cols = slice(j * LANES, (j + 1) * LANES)
            for i in range(2):
                small[0, at + i : at + i + 1, :] = bias_v[t : t + 1, cols]
                small[1, at + i : at + i + 1, :] = out_v[t : t + 1, cols]
            label = labels_v[:, t : t + 1].astype(F32)
            small[2, at : at + 2, :] = jnp.broadcast_to(label, (2, LANES))
            small[3, at : at + 2, :] = jnp.broadcast_to(out_bias_v[:, t : t + 1], (2, LANES))
    loads[0].wait()
    loads[1].wait()
    for t in range(tasks):
        cols = slice(t * width, (t + 1) * width)
        fused[0, :, cols] = dot(w_out_v[...], tower_v[t]).astype(BF)
    fused_copy = remote(fused.at[0], fused.at[1], w_send.at[1], w_recv.at[1], sibling)
    fused_copy.start()
    loads[3].wait()
    same_task = ones_where((gates, gates), lambda r, c: r // experts == c // experts)
    own_share = ones_where(
        (gates, wide), lambda r, c: (r // experts == c // width) & (r % experts == ex)
    )

    def gate_probs(rows):
        logits = dot_nt(rows, gate_v[...])
        lane = lax.broadcasted_iota(jnp.int32, logits.shape, 1) // experts
        top = jnp.zeros_like(logits)
        for t in range(tasks):
            mine = lane == t
            peak = jnp.max(jnp.where(mine, logits, -jnp.inf), axis=1, keepdims=True)
            top = jnp.where(mine, peak, top)
        grown = jnp.exp(logits - top)
        high, low = split(grown)
        return grown / (dot(high, same_task) + dot(low, same_task))

    def shares(probs):
        high, low = split(probs)
        return dot(high, own_share) + dot(low, own_share)

    spread_wait(first_buf, first_send, first_recv)
    unshuffle(first_buf, ev_a.at[chip], feat // LANES)

    def to_chips(buf, send, recv):
        @pl.loop(1, n_chip)
        def _(k):
            mine = buf.at[chip]
            remote(mine, buf.at[chip], send.at[k], recv.at[chip], chip_peer(k)).start()

    def arrived(buf, send, recv, slot):
        remote(buf.at[slot], buf.at[slot], send.at[0], recv.at[slot], sibling).wait_recv()

    def forward(buf, other, send, recv, slot):
        remote(buf.at[slot], other.at[slot], send.at[slot], recv.at[slot], sibling).start()

    def sends_done(buf, send, first, last):
        @pl.loop(first, last)
        def _(k):
            remote(buf.at[0], buf.at[0], send.at[k], send.at[k], sibling).wait_send()

    rows_half = blk // 2
    left = y_lo * n_x + lax.rem(x + n_x - 1, n_x)
    right = y_lo * n_x + lax.rem(x + 1, n_x)
    across = y_lo * n_x + lax.rem(x + 2, n_x)
    other_row = (1 - 2 * y_lo) * n_x

    class Gather:
        def __init__(self, buf, twin, send, recv, twin_send, twin_recv):
            self.buf, self.twin, self.send, self.recv = buf, twin, send, recv
            self.twin_send, self.twin_recv = twin_send, twin_recv

        def half(self, slot, h, buf=None):
            buf = self.buf if buf is None else buf
            return buf.at[slot, pl.ds(h * rows_half, rows_half)]

        def push(self, slot, h, to, sem):
            ref = self.half(slot, h)
            remote(ref, ref, self.send.at[sem], self.recv.at[slot, h], to).start()

        def got(self, slot, h):
            ref = self.half(slot, h)
            remote(ref, ref, self.send.at[0], self.recv.at[slot, h], sibling).wait_recv()

        def pass_on(self, slot, h):
            remote(
                self.half(slot, h),
                self.half(slot, h, self.twin),
                self.twin_send.at[slot, h],
                self.twin_recv.at[slot, h],
                sibling,
            ).start()

        def begin(self):
            self.push(chip, 0, x_peer(1), 0)
            self.push(chip, 1, x_peer(-1), 1)
            self.push(chip, 0, y_peer(1), 2)
            self.push(chip, 1, y_peer(-1), 3)
            self.push(chip, 1, x_peer(1), 4)
            self.push(chip, 0, x_peer(-1), 5)
            self.pass_on(chip, 0)
            self.pass_on(chip, 1)

        def sides(self):
            self.got(left, 0)
            self.push(left, 0, x_peer(1), 6)
            self.push(left, 0, y_peer(1), 7)
            self.got(right, 1)
            self.push(right, 1, x_peer(-1), 8)
            self.push(right, 1, y_peer(-1), 9)
            self.got(left, 1)
            self.push(left, 1, y_peer(-1), 10)
            self.got(right, 0)
            self.push(right, 0, y_peer(1), 11)
            for slot in (left, right):
                self.pass_on(slot, 0)
                self.pass_on(slot, 1)

        def opposite(self):
            self.got(across, 0)
            self.push(across, 0, y_peer(1), 12)
            self.got(across, 1)
            self.push(across, 1, y_peer(-1), 13)
            self.pass_on(across, 0)
            self.pass_on(across, 1)

        def other(self, slot):
            slot = slot + other_row
            for h in range(2):
                self.got(slot, h)
                self.pass_on(slot, h)
            return slot

        def twin_row(self, first):
            @pl.loop(0, n_x)
            def _(k):
                for h in range(2):
                    ref = self.half(first + k, h, self.twin)
                    remote(
                        ref, ref, self.send.at[0], self.twin_recv.at[first + k, h], sibling
                    ).wait_recv()

        def sent(self):
            ref = self.half(0, 0)

            @pl.loop(0, 14)
            def _(k):
                remote(ref, ref, self.send.at[k], self.recv.at[0, 0], sibling).wait_send()

            @pl.loop(0, n_chip)
            def _(k):
                for h in range(2):
                    sem = self.twin_send.at[k, h]
                    remote(ref, ref, sem, self.recv.at[0, 0], sibling).wait_send()

    events = Gather(ev_a, ev_b, ev_send, ev_recv, evf_send, evf_recv)
    events.begin()
    probs = gate_probs(ev_a[chip])
    prob_own[...] = probs
    share_own[...] = shares(probs)
    loads[2].wait()
    w_in_copy.wait_recv()
    fused_copy.wait_recv()

    def forward_block(slot):
        rows = ev_a[slot]
        part = None
        for h in range(2):
            pre = dot(rows, w_in_v[h])
            hidden = gelu_parts(pre)[0].astype(BF)
            term = dot(hidden, fused[h])
            part = term if part is None else part + term
        return part

    def send_part(slot, sem):
        part_send[slot] = forward_block(slot).astype(BF)
        to = (slot * CORES + core, ex)
        remote(
            part_send.at[slot], part_recv.at[chip], part_ssem.at[sem], part_rsem.at[chip], to
        ).start()

    part_own[...] = forward_block(chip)
    events.sides()
    send_part(left, 1)
    send_part(right, 2)
    events.opposite()
    send_part(across, 3)
    send_part(events.other(chip), 4)
    send_part(events.other(left), 5)
    send_part(events.other(right), 6)
    send_part(events.other(across), 7)

    def prepare(group, buf, at):
        rows = buf[pl.ds(at * per_group, per_group)].reshape(g_rows, feat)
        pre = dot(rows, w_in_v[0])
        value, slope = gelu_parts(pre)
        slope_v[group] = slope
        hidden_t[group] = value.T.astype(BF)
        ev_t[group] = rows.astype(F32).T.astype(BF)
        share[group] = shares(gate_probs(rows))

    @pl.loop(0, half)
    def _(g):
        prepare(g, ev_a, g)

    events.twin_row(0)
    events.twin_row(n_x)

    @pl.loop(0, half)
    def _(g):
        prepare(half + g, ev_b, g)

    total = part_own[...]
    for k in range(1, n_chip):
        slot = lax.rem(chip + k, n_chip)
        arrived(part_recv, part_ssem, part_rsem, slot)
        total = total + part_recv[slot].astype(F32)
    terms = total * share_own[...]
    crow = term_send.shape[1]
    for j in range(wide // LANES):
        for i in range(2):
            shuf[pl.ds(j * 2 + i, n_ex, stride=crow), :] = terms[
                i * n_ex : (i + 1) * n_ex, j * LANES : (j + 1) * LANES
            ]
    term_send[...] = shuf[pl.ds(0, n_ex * crow), :].reshape(n_ex, crow, LANES).astype(BF)
    spread(lambda to: term_send.at[to], term_recv, term_ssem, term_rsem)
    term_recv[ex] = term_send[ex]
    spread_wait(term_recv, term_ssem, term_rsem)

    def both_halves(value):
        row = lax.broadcasted_iota(jnp.int32, value.shape, 0)
        step = 2
        while step < 2 * (width // LANES):
            up = pltpu.roll(value, crow - step, 0)
            down = pltpu.roll(value, step, 0)
            value = value + jnp.where((row // step) % 2 == 0, up, down)
            step *= 2
        return value

    mixed = jnp.sum(term_recv[...].astype(F32), axis=0)
    act, act_slope = gelu_parts(mixed + small[0])
    weight = small[1]
    summed = jnp.broadcast_to(jnp.sum(act * weight, axis=1, keepdims=True), mixed.shape)
    logit = both_halves(summed) + small[3]
    dlogit = 1.0 / (1.0 + jnp.exp(-logit)) - small[2]
    dt = (dlogit * weight * act_slope).astype(BF)
    dt_chunk[...] = dt
    spread(lambda _: dt_chunk, dt_first, dt1_send, dt1_recv)
    dt_first[ex] = dt

    prod = (term_recv[...].astype(F32) * dt.astype(F32)[None]).reshape(n_ex * crow, LANES)
    high, low = split(prod)
    all_ones = jnp.ones((LANES, gates), BF)
    sums = dot(high, all_ones) + dot(low, all_ones)
    at = lax.broadcasted_iota(jnp.int32, sums.shape, 0)
    lane = lax.broadcasted_iota(jnp.int32, sums.shape, 1)
    here = lane == (at % crow) // (2 * (width // LANES)) * experts + at // crow
    sums = jnp.where(here, sums, 0.0)
    pick = ones_where((16, n_ex * crow), lambda r, c: (r == c % 2))
    high, low = split(sums)
    moved = dot(pick, high) + dot(pick, low)
    high, low = split(moved)
    weighted = dot(high, same_task) + dot(low, same_task)
    own_rows = jnp.concatenate(
        [
            prob_own[pl.ds(ex, 1), :],
            prob_own[pl.ds(n_ex + ex, 1), :],
            jnp.zeros((14, gates), F32),
        ],
        axis=0,
    )
    dg = (moved - own_rows * weighted).astype(BF)
    dg_chunk[...] = dg
    spread(lambda _: dg_chunk, dg_first, dg1_send, dg1_recv)
    dg_first[ex] = dg

    spread_wait(dt_first, dt1_send, dt1_recv)
    unshuffle(dt_first, dt_a.at[chip], wide // LANES)
    towers = Gather(dt_a, dt_b, dt_send, dt_recv, dtf_send, dtf_recv)
    towers.begin()
    spread_wait(dg_first, dg1_send, dg1_recv)
    rows16 = dg_first.shape[1]
    shuf2 = shuf.at[pl.ds(0, n_ex * rows16)]
    shuf2[:, 0:gates] = dg_first[...].astype(F32).reshape(n_ex * rows16, gates)
    for i in range(2):
        dg_a[chip, i * n_ex : (i + 1) * n_ex, :] = shuf2[pl.ds(i, n_ex, stride=rows16), :][
            :, 0:gates
        ].astype(BF)
    to_chips(dg_a, dg_send, dg_recv)
    forward(dg_a, dg_b, dgf_send, dgf_recv, chip)

    acc_in[...] = jnp.zeros_like(acc_in)
    acc_mid[...] = jnp.zeros_like(acc_mid)
    acc_gate[...] = jnp.zeros_like(acc_gate)

    def backward(group, dt_buf, at):
        span = pl.ds(at * per_group, per_group)
        dout = (dt_buf[span].reshape(g_rows, wide).astype(F32) * share[group]).astype(BF)
        dhidden = dot_nt(dout, fused[0])
        dpre = (dhidden * slope_v[group]).astype(BF)
        acc_in[...] += dot(ev_t[group], dpre)
        acc_mid[...] += dot(hidden_t[group], dout)

    def gate_rows(ev_buf, dg_buf, at):
        span = pl.ds(at * per_group, per_group)
        rows = ev_buf[span].reshape(g_rows, feat)
        acc_gate[...] += dot(dg_buf[span].reshape(g_rows, gates).astype(F32).T.astype(BF), rows)

    towers.sides()
    towers.opposite()
    backward(y_lo, dt_a, y_lo)

    @pl.loop(1, n_chip)
    def _(k):
        slot = lax.rem(chip + k, n_chip)
        arrived(dg_a, dg_send, dg_recv, slot)
        forward(dg_a, dg_b, dgf_send, dgf_recv, slot)

    towers.other(chip)
    towers.other(left)
    towers.other(right)
    towers.twin_row(y_lo * n_x)
    backward(half + y_lo, dt_b, y_lo)
    towers.other(across)
    backward(1 - y_lo, dt_a, 1 - y_lo)

    @pl.loop(0, n_chip)
    def _(k):
        arrived(dg_b, dgf_send, dgf_recv, k)

    for g in range(half):
        gate_rows(ev_a, dg_a, g)
        gate_rows(ev_b, dg_b, g)
    towers.twin_row((1 - y_lo) * n_x)
    backward(half + 1 - y_lo, dt_b, 1 - y_lo)

    grad_in_ref[...] = acc_in[...].astype(BF)
    mid = acc_mid[...].astype(BF)
    result = None
    for t in range(tasks):
        term = dot_nt(mid[:, t * width : (t + 1) * width], tower_v[t])
        result = term if result is None else result + term
    grad_out_ref[...] = result.astype(BF)
    mine = ones_where((16, gates), lambda r, c: (c == r * experts + ex))
    high, low = split(acc_gate[...])
    gate_sums = dot(mine, high) + dot(mine, low)
    for t in range(tasks):
        grad_gate_ref[t] = gate_sums[t : t + 1]

    w_in_copy.wait_send()
    fused_copy.wait_send()
    events.sent()
    towers.sent()
    for buf, send in ((part_send, part_ssem), (dg_a, dg_send)):
        sends_done(buf, send, 1, n_chip)
    sends_done(dg_a, dgf_send, 0, n_chip)


def place(*refs):
    count = (len(refs) - 1) // 2
    sem = refs[-1]
    copies = [
        pltpu.make_async_copy(refs[i], refs[count + i], sem.at[i]) for i in range(count)
    ]
    for copy in copies:
        copy.start()
    for copy in copies:
        copy.wait()


def per_device(
    n_dp,
    n_ex,
    events,
    labels,
    w_in,
    w_out,
    gate_weight,
    tower_in,
    tower_bias,
    tower_out,
    tower_out_bias,
):
    tasks, feat, width = tower_in.shape
    experts = gate_weight.shape[2]
    hid = w_out.shape[1]
    n_chip = n_dp // CORES
    own = events.shape[0]
    blk = own * n_ex
    plane = n_chip * blk
    g_rows = max(plane // 2, blk)
    groups = 2 * plane // g_rows
    wide = tasks * width
    gates = tasks * experts
    chunk = own * feat // LANES
    chunk_t = own * wide // LANES
    chunk_events = events.reshape(own, feat // LANES, LANES).transpose(1, 0, 2).reshape(chunk, LANES)
    vmem = pl.BlockSpec(memory_space=pltpu.VMEM)
    hbm = pl.BlockSpec(memory_space=pltpu.HBM)
    dma = pltpu.SemaphoreType.DMA
    scratch = [
        pltpu.VMEM((n_ex, chunk, LANES), BF),
        pltpu.VMEM((n_ex * max(chunk, chunk_t, 16), LANES), F32),
        pltpu.VMEM((n_chip, blk, feat), BF),
        pltpu.VMEM((n_chip, blk, feat), BF),
        pltpu.VMEM((2, feat, hid), BF),
        pltpu.VMEM((hid, feat), BF),
        pltpu.VMEM((2, hid, wide), BF),
        pltpu.VMEM((tasks, feat, width), BF),
        pltpu.VMEM((gates, feat), BF),
        pltpu.VMEM((own, tasks), jnp.int32),
        pltpu.VMEM((tasks, width), F32),
        pltpu.VMEM((tasks, width), F32),
        pltpu.VMEM((1, tasks), F32),
        pltpu.VMEM((blk, wide), F32),
        pltpu.VMEM((n_chip, blk, wide), BF),
        pltpu.VMEM((n_chip, blk, wide), BF),
        pltpu.VMEM((n_ex, chunk_t, LANES), BF),
        pltpu.VMEM((n_ex, chunk_t, LANES), BF),
        pltpu.VMEM((4, chunk_t, LANES), F32),
        pltpu.VMEM((blk, gates), F32),
        pltpu.VMEM((blk, wide), F32),
        pltpu.VMEM((groups, g_rows, wide), F32),
        pltpu.VMEM((groups, g_rows, hid), F32),
        pltpu.VMEM((groups, hid, g_rows), BF),
        pltpu.VMEM((groups, feat, g_rows), BF),
        pltpu.VMEM((chunk_t, LANES), BF),
        pltpu.VMEM((n_ex, chunk_t, LANES), BF),
        pltpu.VMEM((n_chip, blk, wide), BF),
        pltpu.VMEM((n_chip, blk, wide), BF),
        pltpu.VMEM((16, gates), BF),
        pltpu.VMEM((n_ex, 16, gates), BF),
        pltpu.VMEM((n_chip, blk, gates), BF),
        pltpu.VMEM((n_chip, blk, gates), BF),
        pltpu.VMEM((feat, hid), F32),
        pltpu.VMEM((hid, wide), F32),
        pltpu.VMEM((gates, feat), F32),
        dma((9,)),
        dma((2,)),
        dma((2,)),
        dma,
        dma,
        dma((14,)),
        dma((n_chip, 2)),
        dma((n_chip, 2)),
        dma((n_chip, 2)),
        dma((n_chip,)),
        dma((n_chip,)),
        dma,
        dma,
        dma,
        dma,
        dma,
        dma,
        dma((14,)),
        dma((n_chip, 2)),
        dma((n_chip, 2)),
        dma((n_chip, 2)),
        dma((n_chip,)),
        dma((n_chip,)),
        dma((n_chip,)),
        dma((n_chip,)),
    ]
    results = pl.pallas_call(
        functools.partial(kernel, n_ex, n_chip, tasks, width),
        out_shape=(
            jax.ShapeDtypeStruct((feat, hid), BF),
            jax.ShapeDtypeStruct((hid, feat), BF),
            jax.ShapeDtypeStruct((tasks, 1, feat), F32),
        ),
        in_specs=[hbm] * 9,
        out_specs=(vmem, vmem, vmem),
        scratch_shapes=scratch,
        compiler_params=pltpu.CompilerParams(
            collective_id=0, has_side_effects=True, vmem_limit_bytes=VMEM_MIB * 1024 * 1024
        ),
    )(
        *(
            pltpu.with_memory_space_constraint(operand, pltpu.HBM)
            for operand in (
                chunk_events,
                labels,
                w_in,
                w_out,
                gate_weight.transpose(0, 2, 1).reshape(gates, feat),
                tower_in,
                tower_bias,
                tower_out,
                tower_out_bias.reshape(1, tasks),
            )
        )
    )
    grad_in, grad_out, grad_gate = pl.pallas_call(
        place,
        out_shape=[jax.ShapeDtypeStruct(r.shape, r.dtype) for r in results],
        in_specs=[pl.BlockSpec(memory_space=pl.ANY)] * len(results),
        out_specs=[hbm] * len(results),
        scratch_shapes=[dma((len(results),))],
    )(*results)
    return grad_in[None], grad_out[None], grad_gate.transpose(0, 2, 1)


def solution(mesh):
    placed = (
        P(("dp", "expert"), None),
        P(("dp", "expert"), None),
        P("expert", None, "dp"),
        P("expert", "dp", None),
        P(),
        P(),
        P(),
        P(),
        P(),
    )
    return jax.shard_map(
        functools.partial(per_device, mesh.shape["dp"], mesh.shape["expert"]),
        mesh=mesh,
        in_specs=placed,
        out_specs=(P("expert", None, "dp"), P("expert", "dp", None), P(None, None, "expert")),
        check_vma=False,
    )
```

```python
import functools
import math

import jax
import jax.numpy as jnp
from jax import lax
from jax.experimental import pallas as pl
from jax.experimental.pallas import tpu as pltpu
from jax.sharding import PartitionSpec as P

MESH = pl.DeviceIdType.MESH
BF = jnp.bfloat16
F32 = jnp.float32
LANES = 128
CORES = 2
GELU_A = math.sqrt(2.0 / math.pi)
GELU_B = 0.044715
VMEM_MIB = 34
EV_PARTS = 2
DT_PARTS = 2


def dot(a, b):
    return jnp.dot(a, b, preferred_element_type=F32)


def dot_nt(a, b):
    return lax.dot_general(a, b, (((1,), (1,)), ((), ())), preferred_element_type=F32)


def dot_tn(a, b):
    return lax.dot_general(a, b, (((0,), (0,)), ((), ())), preferred_element_type=F32)


def split(a):
    high = a.astype(BF)
    return high, (a - high.astype(F32)).astype(BF)


def gelu_parts(x):
    t = jnp.tanh(GELU_A * (x + GELU_B * x * x * x))
    value = 0.5 * x * (1.0 + t)
    slope = 0.5 * (1.0 + t) + 0.5 * x * (1.0 - t * t) * GELU_A * (1.0 + 3.0 * GELU_B * x * x)
    return value, slope


def ones_where(shape, test):
    rows = lax.broadcasted_iota(jnp.int32, shape, 0)
    cols = lax.broadcasted_iota(jnp.int32, shape, 1)
    return jnp.where(test(rows, cols), 1.0, 0.0).astype(BF)


def kernel(
    n_ex,
    n_chip,
    tasks,
    width,
    own_hbm,
    labels_hbm,
    w_in_hbm,
    w_out_hbm,
    gate_hbm,
    tower_hbm,
    bias_hbm,
    out_hbm,
    out_bias_hbm,
    grad_in_ref,
    grad_out_ref,
    grad_gate_ref,
    first_buf,
    shuf,
    ev_a,
    ev_b,
    w_in_v,
    w_out_v,
    fused,
    tower_v,
    gate_v,
    labels_v,
    bias_v,
    out_v,
    out_bias_v,
    part_own,
    part_send,
    part_recv,
    term_send,
    term_recv,
    small,
    prob_own,
    share_own,
    share,
    slope_v,
    hidden_t,
    ev_t,
    dt_chunk,
    dt_first,
    dt_a,
    dt_b,
    dg_chunk,
    dg_first,
    dg_a,
    dg_b,
    acc_in,
    acc_mid,
    acc_gate,
    load_sem,
    w_send,
    w_recv,
    first_send,
    first_recv,
    ev_send,
    ev_recv,
    evf_send,
    evf_recv,
    part_ssem,
    part_rsem,
    term_ssem,
    term_rsem,
    dt1_send,
    dt1_recv,
    dg1_send,
    dg1_recv,
    dt_send,
    dt_recv,
    dtf_send,
    dtf_recv,
    dg_send,
    dg_recv,
    dgf_send,
    dgf_recv,
):
    dp = lax.axis_index("dp")
    ex = lax.axis_index("expert")
    core = lax.rem(dp, CORES)
    chip = lax.div(dp, CORES)
    n_x = n_chip // 2
    n_yh = min(4, n_ex)
    n_z = n_ex // n_yh
    x, y_lo = lax.rem(chip, n_x), lax.div(chip, n_x)
    y_hi, z = lax.div(ex, n_z), lax.rem(ex, n_z)
    y = y_hi * 2 + y_lo
    sibling = (dp + 1 - 2 * core, ex)
    feat = ev_a.shape[2]
    wide = tasks * width
    blk = ev_a.shape[1]
    hid = w_out_v.shape[0]
    gates = gate_v.shape[0]
    experts = gates // tasks
    g_rows = ev_t.shape[2]
    per_group = g_rows // blk
    half = n_chip // per_group

    def ex_peer(k):
        return (dp, lax.rem(ex + k, n_ex))

    def chip_peer(k):
        return (lax.rem(chip + k, n_chip) * CORES + core, ex)

    def x_peer(step):
        return ((y_lo * n_x + lax.rem(x + step + n_x, n_x)) * CORES + core, ex)

    def y_peer(step):
        to = lax.rem(y + step + 2 * n_yh, 2 * n_yh)
        return (
            (lax.rem(to, 2) * n_x + x) * CORES + core,
            lax.div(to, 2) * n_z + lax.rem(ex, n_z),
        )

    def remote(src, dst, send, recv, to):
        return pltpu.make_async_remote_copy(
            src_ref=src, dst_ref=dst, send_sem=send, recv_sem=recv, device_id=to, device_id_type=MESH
        )

    barrier = pltpu.get_barrier_semaphore()

    @pl.loop(1, n_ex)
    def _(k):
        pl.semaphore_signal(barrier, inc=1, device_id=ex_peer(k), device_id_type=MESH)

    @pl.loop(1, n_chip)
    def _(k):
        pl.semaphore_signal(barrier, inc=1, device_id=chip_peer(k), device_id_type=MESH)

    pl.semaphore_signal(barrier, inc=1, device_id=sibling, device_id_type=MESH)
    pl.semaphore_signal(barrier, inc=1, device_id=y_peer(2 * y_lo - 1), device_id_type=MESH)

    loads = [
        pltpu.make_async_copy(src, dst, load_sem.at[i])
        for i, (src, dst) in enumerate(
            (
                (w_out_hbm.at[0], w_out_v),
                (tower_hbm, tower_v),
                (w_in_hbm.at[0], w_in_v.at[0]),
                (gate_hbm, gate_v),
                (labels_hbm, labels_v),
                (bias_hbm, bias_v),
                (out_hbm, out_v),
                (out_bias_hbm, out_bias_v),
                (own_hbm, first_buf.at[ex]),
            )
        )
    ]
    for load in loads:
        load.start()
    pl.semaphore_wait(barrier, n_ex + n_chip)

    steps = [(a, b) for a in range(n_yh) for b in range(n_z) if a or b]
    steps.sort(key=lambda s: -(2 * min(s[0], n_yh - s[0]) + min(s[1], n_z - s[1])))

    def spread(src_of, dst, send, recv):
        for a, b in steps:
            to_ex = lax.rem(y_hi + a, n_yh) * n_z + lax.rem(z + b, n_z)
            remote(src_of(to_ex), dst.at[ex], send, recv, (dp, to_ex)).start()

    def spread_wait(dst, send, recv):
        every = dst.at[pl.ds(0, n_ex - 1)]
        copy = remote(every, every, send, recv, ex_peer(1))
        copy.wait_recv()
        copy.wait_send()

    def unshuffle(src, dst, count):
        rows = src.shape[1]
        shuf[pl.ds(0, n_ex * rows), :] = src[...].astype(F32).reshape(n_ex * rows, LANES)
        for j in range(count):
            for i in range(2):
                piece = shuf[pl.ds(j * 2 + i, n_ex, stride=rows), :]
                dst[i * n_ex : (i + 1) * n_ex, j * LANES : (j + 1) * LANES] = piece.astype(BF)

    spread(lambda _: own_hbm, first_buf, first_send, first_recv)
    w_in_copy = remote(w_in_hbm.at[0], w_in_v.at[1], w_send.at[0], w_recv.at[0], sibling)
    w_in_copy.start()
    for load in loads[4:9]:
        load.wait()
    for t in range(tasks):
        for j in range(width // LANES):
            at = (t * (width // LANES) + j) * 2
            cols = slice(j * LANES, (j + 1) * LANES)
            for i in range(2):
                small[0, at + i : at + i + 1, :] = bias_v[t : t + 1, cols]
                small[1, at + i : at + i + 1, :] = out_v[t : t + 1, cols]
            label = labels_v[:, t : t + 1].astype(F32)
            small[2, at : at + 2, :] = jnp.broadcast_to(label, (2, LANES))
            small[3, at : at + 2, :] = jnp.broadcast_to(out_bias_v[:, t : t + 1], (2, LANES))
    loads[0].wait()
    loads[1].wait()
    for t in range(tasks):
        cols = slice(t * width, (t + 1) * width)
        fused[0, :, cols] = dot(w_out_v[...], tower_v[t]).astype(BF)
    fused_copy = remote(fused.at[0], fused.at[1], w_send.at[1], w_recv.at[1], sibling)
    fused_copy.start()
    loads[3].wait()
    same_task = ones_where((gates, gates), lambda r, c: r // experts == c // experts)
    own_share = ones_where(
        (gates, wide), lambda r, c: (r // experts == c // width) & (r % experts == ex)
    )

    def gate_probs(rows):
        logits = dot_nt(rows, gate_v[...])
        lane = lax.broadcasted_iota(jnp.int32, logits.shape, 1) // experts
        top = jnp.zeros_like(logits)
        for t in range(tasks):
            mine = lane == t
            peak = jnp.max(jnp.where(mine, logits, -jnp.inf), axis=1, keepdims=True)
            top = jnp.where(mine, peak, top)
        grown = jnp.exp(logits - top)
        high, low = split(grown)
        return grown / (dot(high, same_task) + dot(low, same_task))

    def shares(probs):
        high, low = split(probs)
        return dot(high, own_share) + dot(low, own_share)

    spread_wait(first_buf, first_send, first_recv)
    unshuffle(first_buf, ev_a.at[chip], feat // LANES)

    def to_chips(buf, send, recv):
        @pl.loop(1, n_chip)
        def _(k):
            mine = buf.at[chip]
            remote(mine, buf.at[chip], send.at[k], recv.at[chip], chip_peer(k)).start()

    def arrived(buf, send, recv, slot):
        remote(buf.at[slot], buf.at[slot], send.at[0], recv.at[slot], sibling).wait_recv()

    def forward(buf, other, send, recv, slot):
        remote(buf.at[slot], other.at[slot], send.at[slot], recv.at[slot], sibling).start()

    def sends_done(buf, send, first, last):
        @pl.loop(first, last)
        def _(k):
            remote(buf.at[0], buf.at[0], send.at[k], send.at[k], sibling).wait_send()

    left = y_lo * n_x + lax.rem(x + n_x - 1, n_x)
    right = y_lo * n_x + lax.rem(x + 1, n_x)
    across = y_lo * n_x + lax.rem(x + 2, n_x)
    other_row = (1 - 2 * y_lo) * n_x

    class Gather:
        def __init__(self, parts, buf, twin, send, recv, twin_send, twin_recv):
            self.buf, self.twin, self.send, self.recv = buf, twin, send, recv
            self.twin_send, self.twin_recv = twin_send, twin_recv
            self.rows = blk // parts
            self.up = list(range(parts // 2))
            self.down = list(range(parts // 2, parts))
            self.count = 0

        def part(self, slot, p):
            return self.buf.at[slot, pl.ds(p * self.rows, self.rows)]

        def push(self, slot, p, to):
            ref = self.part(slot, p)
            remote(ref, ref, self.send.at[self.count], self.recv.at[slot, p], to).start()
            self.count += 1

        def got(self, slot, p):
            ref = self.part(slot, p)
            remote(ref, ref, self.send.at[0], self.recv.at[slot, p], sibling).wait_recv()

        def pass_on(self, slot):
            remote(
                self.buf.at[slot],
                self.twin.at[slot],
                self.twin_send.at[slot],
                self.twin_recv.at[slot],
                sibling,
            ).start()

        def begin(self):
            for u, d in zip(self.up, self.down):
                self.push(chip, u, x_peer(1))
                self.push(chip, d, x_peer(-1))
                self.push(chip, u, y_peer(1))
                self.push(chip, d, y_peer(-1))
            for u, d in zip(self.up, self.down):
                self.push(chip, d, x_peer(1))
                self.push(chip, u, x_peer(-1))
            self.pass_on(chip)

        def sides(self):
            for u, d in zip(self.up, self.down):
                self.got(left, u)
                self.push(left, u, x_peer(1))
                self.push(left, u, y_peer(1))
                self.got(right, d)
                self.push(right, d, x_peer(-1))
                self.push(right, d, y_peer(-1))
            for u, d in zip(self.up, self.down):
                self.got(left, d)
                self.push(left, d, y_peer(-1))
                self.got(right, u)
                self.push(right, u, y_peer(1))
            self.pass_on(left)
            self.pass_on(right)

        def opposite(self):
            for u, d in zip(self.up, self.down):
                self.got(across, u)
                self.push(across, u, y_peer(1))
                self.got(across, d)
                self.push(across, d, y_peer(-1))
            self.pass_on(across)

        def other(self, slot):
            slot = slot + other_row
            for p in self.up + self.down:
                self.got(slot, p)
            self.pass_on(slot)
            return slot

        def twin_row(self, first):
            @pl.loop(0, n_x)
            def _(k):
                arrived(self.twin, self.send, self.twin_recv, first + k)

        def sent(self):
            ref = self.part(0, 0)

            @pl.loop(0, self.count)
            def _(k):
                remote(ref, ref, self.send.at[k], self.recv.at[0, 0], sibling).wait_send()

            sends_done(self.buf, self.twin_send, 0, n_chip)

    events = Gather(EV_PARTS, ev_a, ev_b, ev_send, ev_recv, evf_send, evf_recv)
    events.begin()
    probs = gate_probs(ev_a[chip])
    prob_own[...] = probs
    share_own[...] = shares(probs)
    loads[2].wait()
    w_in_copy.wait_recv()
    fused_copy.wait_recv()

    def forward_block(slot):
        rows = ev_a[slot]
        part = None
        for h in range(2):
            pre = dot(rows, w_in_v[h])
            hidden = gelu_parts(pre)[0].astype(BF)
            term = dot(hidden, fused[h])
            part = term if part is None else part + term
        return part

    def send_part(slot, sem):
        part_send[slot] = forward_block(slot).astype(BF)
        to = (slot * CORES + core, ex)
        remote(
            part_send.at[slot], part_recv.at[chip], part_ssem.at[sem], part_rsem.at[chip], to
        ).start()

    part_own[...] = forward_block(chip)
    send_part(events.other(chip), 4)
    events.sides()
    send_part(left, 1)
    send_part(right, 2)
    events.opposite()
    send_part(across, 3)
    send_part(events.other(left), 5)
    send_part(events.other(right), 6)
    send_part(events.other(across), 7)

    def prepare(group, buf, at):
        rows = buf[pl.ds(at * per_group, per_group)].reshape(g_rows, feat)
        pre = dot(rows, w_in_v[0])
        value, slope = gelu_parts(pre)
        slope_v[group] = slope
        hidden_t[group] = value.T.astype(BF)
        ev_t[group] = rows.astype(F32).T.astype(BF)
        share[group] = shares(gate_probs(rows))

    @pl.loop(0, half)
    def _(g):
        prepare(g, ev_a, g)

    events.twin_row(0)
    events.twin_row(n_x)

    @pl.loop(0, half)
    def _(g):
        prepare(half + g, ev_b, g)

    total = part_own[...]
    for k in range(1, n_chip):
        slot = lax.rem(chip + k, n_chip)
        arrived(part_recv, part_ssem, part_rsem, slot)
        total = total + part_recv[slot].astype(F32)
    terms = total * share_own[...]
    crow = term_send.shape[1]
    for j in range(wide // LANES):
        for i in range(2):
            shuf[pl.ds(j * 2 + i, n_ex, stride=crow), :] = terms[
                i * n_ex : (i + 1) * n_ex, j * LANES : (j + 1) * LANES
            ]
    term_send[...] = shuf[pl.ds(0, n_ex * crow), :].reshape(n_ex, crow, LANES).astype(BF)
    spread(lambda to: term_send.at[to], term_recv, term_ssem, term_rsem)
    term_recv[ex] = term_send[ex]
    spread_wait(term_recv, term_ssem, term_rsem)

    def both_halves(value):
        row = lax.broadcasted_iota(jnp.int32, value.shape, 0)
        step = 2
        while step < 2 * (width // LANES):
            up = pltpu.roll(value, crow - step, 0)
            down = pltpu.roll(value, step, 0)
            value = value + jnp.where((row // step) % 2 == 0, up, down)
            step *= 2
        return value

    mixed = jnp.sum(term_recv[...].astype(F32), axis=0)
    act, act_slope = gelu_parts(mixed + small[0])
    weight = small[1]
    summed = jnp.broadcast_to(jnp.sum(act * weight, axis=1, keepdims=True), mixed.shape)
    logit = both_halves(summed) + small[3]
    dlogit = 1.0 / (1.0 + jnp.exp(-logit)) - small[2]
    dt = (dlogit * weight * act_slope).astype(BF)
    dt_chunk[...] = dt
    spread(lambda _: dt_chunk, dt_first, dt1_send, dt1_recv)
    dt_first[ex] = dt

    prod = (term_recv[...].astype(F32) * dt.astype(F32)[None]).reshape(n_ex * crow, LANES)
    high, low = split(prod)
    all_ones = jnp.ones((LANES, gates), BF)
    sums = dot(high, all_ones) + dot(low, all_ones)
    at = lax.broadcasted_iota(jnp.int32, sums.shape, 0)
    lane = lax.broadcasted_iota(jnp.int32, sums.shape, 1)
    here = lane == (at % crow) // (2 * (width // LANES)) * experts + at // crow
    sums = jnp.where(here, sums, 0.0)
    pick = ones_where((16, n_ex * crow), lambda r, c: (r == c % 2))
    high, low = split(sums)
    moved = dot(pick, high) + dot(pick, low)
    high, low = split(moved)
    weighted = dot(high, same_task) + dot(low, same_task)
    own_rows = jnp.concatenate(
        [
            prob_own[pl.ds(ex, 1), :],
            prob_own[pl.ds(n_ex + ex, 1), :],
            jnp.zeros((14, gates), F32),
        ],
        axis=0,
    )
    dg = (moved - own_rows * weighted).astype(BF)
    dg_chunk[...] = dg
    spread(lambda _: dg_chunk, dg_first, dg1_send, dg1_recv)
    dg_first[ex] = dg

    spread_wait(dt_first, dt1_send, dt1_recv)
    unshuffle(dt_first, dt_a.at[chip], wide // LANES)
    towers = Gather(DT_PARTS, dt_a, dt_b, dt_send, dt_recv, dtf_send, dtf_recv)
    towers.begin()
    spread_wait(dg_first, dg1_send, dg1_recv)
    rows16 = dg_first.shape[1]
    shuf2 = shuf.at[pl.ds(0, n_ex * rows16)]
    shuf2[:, 0:gates] = dg_first[...].astype(F32).reshape(n_ex * rows16, gates)
    for i in range(2):
        dg_a[chip, i * n_ex : (i + 1) * n_ex, :] = shuf2[pl.ds(i, n_ex, stride=rows16), :][
            :, 0:gates
        ].astype(BF)
    to_chips(dg_a, dg_send, dg_recv)
    forward(dg_a, dg_b, dgf_send, dgf_recv, chip)

    acc_in[...] = jnp.zeros_like(acc_in)
    acc_mid[...] = jnp.zeros_like(acc_mid)
    acc_gate[...] = jnp.zeros_like(acc_gate)

    def backward(group, dt_buf, at):
        span = pl.ds(at * per_group, per_group)
        dout = (dt_buf[span].reshape(g_rows, wide).astype(F32) * share[group]).astype(BF)
        dhidden = dot_nt(dout, fused[0])
        dpre = (dhidden * slope_v[group]).astype(BF)
        acc_in[...] += dot(ev_t[group], dpre)
        acc_mid[...] += dot(hidden_t[group], dout)

    def gate_rows(ev_buf, dg_buf, at):
        span = pl.ds(at * per_group, per_group)
        rows = ev_buf[span].reshape(g_rows, feat)
        acc_gate[...] += dot(dg_buf[span].reshape(g_rows, gates).astype(F32).T.astype(BF), rows)

    towers.sides()

    @pl.loop(1, n_chip)
    def _(k):
        slot = lax.rem(chip + k, n_chip)
        arrived(dg_a, dg_send, dg_recv, slot)
        forward(dg_a, dg_b, dgf_send, dgf_recv, slot)

    for g in range(half):
        gate_rows(ev_a, dg_a, g)
    towers.opposite()
    backward(y_lo, dt_a, y_lo)
    towers.other(chip)
    towers.other(left)
    towers.other(right)
    towers.twin_row(y_lo * n_x)
    backward(half + y_lo, dt_b, y_lo)

    @pl.loop(0, n_chip)
    def _(k):
        arrived(dg_b, dgf_send, dgf_recv, k)

    for g in range(half):
        gate_rows(ev_b, dg_b, g)
    towers.other(across)
    backward(1 - y_lo, dt_a, 1 - y_lo)
    mine = ones_where((16, gates), lambda r, c: (c == r * experts + ex))
    high, low = split(acc_gate[...])
    gate_sums = dot(mine, high) + dot(mine, low)
    for t in range(tasks):
        grad_gate_ref[t] = gate_sums[t : t + 1]
    towers.twin_row((1 - y_lo) * n_x)
    backward(half + 1 - y_lo, dt_b, 1 - y_lo)

    grad_in_ref[...] = acc_in[...].astype(BF)
    mid = acc_mid[...].astype(BF)
    result = None
    for t in range(tasks):
        term = dot_nt(mid[:, t * width : (t + 1) * width], tower_v[t])
        result = term if result is None else result + term
    grad_out_ref[...] = result.astype(BF)
    w_in_copy.wait_send()
    fused_copy.wait_send()
    events.sent()
    towers.sent()
    for buf, send in ((part_send, part_ssem), (dg_a, dg_send)):
        sends_done(buf, send, 1, n_chip)
    sends_done(dg_a, dgf_send, 0, n_chip)


def per_device(
    n_dp,
    n_ex,
    events,
    labels,
    w_in,
    w_out,
    gate_weight,
    tower_in,
    tower_bias,
    tower_out,
    tower_out_bias,
):
    tasks, feat, width = tower_in.shape
    experts = gate_weight.shape[2]
    hid = w_out.shape[1]
    n_chip = n_dp // CORES
    own = events.shape[0]
    blk = own * n_ex
    plane = n_chip * blk
    g_rows = max(plane // 2, blk)
    groups = 2 * plane // g_rows
    wide = tasks * width
    gates = tasks * experts
    chunk = own * feat // LANES
    chunk_t = own * wide // LANES
    chunk_events = events.reshape(own, feat // LANES, LANES).transpose(1, 0, 2).reshape(chunk, LANES)
    vmem = pl.BlockSpec(memory_space=pltpu.VMEM)
    hbm = pl.BlockSpec(memory_space=pltpu.HBM)
    dma = pltpu.SemaphoreType.DMA
    scratch = [
        pltpu.VMEM((n_ex, chunk, LANES), BF),
        pltpu.VMEM((n_ex * max(chunk, chunk_t, 16), LANES), F32),
        pltpu.VMEM((n_chip, blk, feat), BF),
        pltpu.VMEM((n_chip, blk, feat), BF),
        pltpu.VMEM((2, feat, hid), BF),
        pltpu.VMEM((hid, feat), BF),
        pltpu.VMEM((2, hid, wide), BF),
        pltpu.VMEM((tasks, feat, width), BF),
        pltpu.VMEM((gates, feat), BF),
        pltpu.VMEM((own, tasks), jnp.int32),
        pltpu.VMEM((tasks, width), F32),
        pltpu.VMEM((tasks, width), F32),
        pltpu.VMEM((1, tasks), F32),
        pltpu.VMEM((blk, wide), F32),
        pltpu.VMEM((n_chip, blk, wide), BF),
        pltpu.VMEM((n_chip, blk, wide), BF),
        pltpu.VMEM((n_ex, chunk_t, LANES), BF),
        pltpu.VMEM((n_ex, chunk_t, LANES), BF),
        pltpu.VMEM((4, chunk_t, LANES), F32),
        pltpu.VMEM((blk, gates), F32),
        pltpu.VMEM((blk, wide), F32),
        pltpu.VMEM((groups, g_rows, wide), F32),
        pltpu.VMEM((groups, g_rows, hid), F32),
        pltpu.VMEM((groups, hid, g_rows), BF),
        pltpu.VMEM((groups, feat, g_rows), BF),
        pltpu.VMEM((chunk_t, LANES), BF),
        pltpu.VMEM((n_ex, chunk_t, LANES), BF),
        pltpu.VMEM((n_chip, blk, wide), BF),
        pltpu.VMEM((n_chip, blk, wide), BF),
        pltpu.VMEM((16, gates), BF),
        pltpu.VMEM((n_ex, 16, gates), BF),
        pltpu.VMEM((n_chip, blk, gates), BF),
        pltpu.VMEM((n_chip, blk, gates), BF),
        pltpu.VMEM((feat, hid), F32),
        pltpu.VMEM((hid, wide), F32),
        pltpu.VMEM((gates, feat), F32),
        dma((9,)),
        dma((2,)),
        dma((2,)),
        dma,
        dma,
        dma((7 * EV_PARTS,)),
        dma((n_chip, EV_PARTS)),
        dma((n_chip,)),
        dma((n_chip,)),
        dma((n_chip,)),
        dma((n_chip,)),
        dma,
        dma,
        dma,
        dma,
        dma,
        dma,
        dma((7 * DT_PARTS,)),
        dma((n_chip, DT_PARTS)),
        dma((n_chip,)),
        dma((n_chip,)),
        dma((n_chip,)),
        dma((n_chip,)),
        dma((n_chip,)),
        dma((n_chip,)),
    ]
    grad_in, grad_out, grad_gate = pl.pallas_call(
        functools.partial(kernel, n_ex, n_chip, tasks, width),
        out_shape=(
            jax.ShapeDtypeStruct((feat, hid), BF),
            jax.ShapeDtypeStruct((hid, feat), BF),
            jax.ShapeDtypeStruct((tasks, 1, feat), F32),
        ),
        in_specs=[hbm] * 9,
        out_specs=(vmem, vmem, vmem),
        scratch_shapes=scratch,
        compiler_params=pltpu.CompilerParams(
            collective_id=0, has_side_effects=True, vmem_limit_bytes=VMEM_MIB * 1024 * 1024
        ),
    )(
        *(
            pltpu.with_memory_space_constraint(operand, pltpu.HBM)
            for operand in (
                chunk_events,
                labels,
                w_in,
                w_out,
                gate_weight.transpose(0, 2, 1).reshape(gates, feat),
                tower_in,
                tower_bias,
                tower_out,
                tower_out_bias.reshape(1, tasks),
            )
        )
    )
    return grad_in[None], grad_out[None], grad_gate.transpose(0, 2, 1)


def solution(mesh):
    placed = (
        P(("dp", "expert"), None),
        P(("dp", "expert"), None),
        P("expert", None, "dp"),
        P("expert", "dp", None),
        P(),
        P(),
        P(),
        P(),
        P(),
    )
    return jax.shard_map(
        functools.partial(per_device, mesh.shape["dp"], mesh.shape["expert"]),
        mesh=mesh,
        in_specs=placed,
        out_specs=(P("expert", None, "dp"), P("expert", "dp", None), P(None, None, "expert")),
        check_vma=False,
    )
```

```python
import functools
import math

import jax
import jax.numpy as jnp
from jax import lax
from jax.experimental import pallas as pl
from jax.experimental.pallas import tpu as pltpu
from jax.sharding import PartitionSpec as P

MESH = pl.DeviceIdType.MESH
BF = jnp.bfloat16
F32 = jnp.float32
LANES = 128
CORES = 2
GELU_A = math.sqrt(2.0 / math.pi)
GELU_B = 0.044715
VMEM_MIB = 34
EV_PARTS = 2
DT_PARTS = 2


def dot(a, b):
    return jnp.dot(a, b, preferred_element_type=F32)


def dot_nt(a, b):
    return lax.dot_general(a, b, (((1,), (1,)), ((), ())), preferred_element_type=F32)


def dot_tn(a, b):
    return lax.dot_general(a, b, (((0,), (0,)), ((), ())), preferred_element_type=F32)


def split(a):
    high = a.astype(BF)
    return high, (a - high.astype(F32)).astype(BF)


def gelu_parts(x):
    t = jnp.tanh(GELU_A * (x + GELU_B * x * x * x))
    value = 0.5 * x * (1.0 + t)
    slope = 0.5 * (1.0 + t) + 0.5 * x * (1.0 - t * t) * GELU_A * (1.0 + 3.0 * GELU_B * x * x)
    return value, slope


def ones_where(shape, test):
    rows = lax.broadcasted_iota(jnp.int32, shape, 0)
    cols = lax.broadcasted_iota(jnp.int32, shape, 1)
    return jnp.where(test(rows, cols), 1.0, 0.0).astype(BF)


def kernel(
    n_ex,
    n_chip,
    tasks,
    width,
    own_hbm,
    labels_hbm,
    w_in_hbm,
    w_out_hbm,
    gate_hbm,
    tower_hbm,
    bias_hbm,
    out_hbm,
    out_bias_hbm,
    grad_in_ref,
    grad_out_ref,
    grad_gate_ref,
    first_buf,
    shuf,
    ev_a,
    ev_b,
    w_in_v,
    w_out_v,
    fused,
    tower_v,
    gate_v,
    labels_v,
    bias_v,
    out_v,
    out_bias_v,
    part_own,
    part_send,
    part_recv,
    term_send,
    term_recv,
    small,
    prob_own,
    share_own,
    share,
    slope_v,
    hidden_t,
    ev_t,
    dt_chunk,
    dt_first,
    dt_a,
    dt_b,
    dg_chunk,
    dg_first,
    dg_a,
    dg_b,
    acc_in,
    acc_mid,
    acc_gate,
    load_sem,
    w_send,
    w_recv,
    first_send,
    first_recv,
    ev_send,
    ev_recv,
    evf_send,
    evf_recv,
    part_ssem,
    part_rsem,
    term_ssem,
    term_rsem,
    dt1_send,
    dt1_recv,
    dg1_send,
    dg1_recv,
    dt_send,
    dt_recv,
    dtf_send,
    dtf_recv,
    dg_send,
    dg_recv,
    dgf_send,
    dgf_recv,
):
    dp = lax.axis_index("dp")
    ex = lax.axis_index("expert")
    core = lax.rem(dp, CORES)
    chip = lax.div(dp, CORES)
    n_x = n_chip // 2
    n_yh = min(4, n_ex)
    n_z = n_ex // n_yh
    x, y_lo = lax.rem(chip, n_x), lax.div(chip, n_x)
    y_hi, z = lax.div(ex, n_z), lax.rem(ex, n_z)
    y = y_hi * 2 + y_lo
    sibling = (dp + 1 - 2 * core, ex)
    feat = ev_a.shape[2]
    wide = tasks * width
    blk = ev_a.shape[1]
    hid = w_out_v.shape[0]
    gates = gate_v.shape[0]
    experts = gates // tasks
    g_rows = ev_t.shape[2]
    per_group = g_rows // blk
    half = n_chip // per_group

    def ex_peer(k):
        return (dp, lax.rem(ex + k, n_ex))

    def chip_peer(k):
        return (lax.rem(chip + k, n_chip) * CORES + core, ex)

    def x_peer(step):
        return ((y_lo * n_x + lax.rem(x + step + n_x, n_x)) * CORES + core, ex)

    def y_peer(step):
        to = lax.rem(y + step + 2 * n_yh, 2 * n_yh)
        return (
            (lax.rem(to, 2) * n_x + x) * CORES + core,
            lax.div(to, 2) * n_z + lax.rem(ex, n_z),
        )

    def remote(src, dst, send, recv, to):
        return pltpu.make_async_remote_copy(
            src_ref=src, dst_ref=dst, send_sem=send, recv_sem=recv, device_id=to, device_id_type=MESH
        )

    own_load = pltpu.make_async_copy(own_hbm, first_buf.at[ex], load_sem.at[8])
    own_load.start()
    barrier = pltpu.get_barrier_semaphore()

    @pl.loop(1, n_ex)
    def _(k):
        pl.semaphore_signal(barrier, inc=1, device_id=ex_peer(k), device_id_type=MESH)

    @pl.loop(1, n_chip)
    def _(k):
        pl.semaphore_signal(barrier, inc=1, device_id=chip_peer(k), device_id_type=MESH)

    pl.semaphore_signal(barrier, inc=1, device_id=sibling, device_id_type=MESH)
    pl.semaphore_signal(barrier, inc=1, device_id=y_peer(2 * y_lo - 1), device_id_type=MESH)

    loads = [
        pltpu.make_async_copy(src, dst, load_sem.at[i])
        for i, (src, dst) in enumerate(
            (
                (w_out_hbm.at[0], w_out_v),
                (tower_hbm, tower_v),
                (w_in_hbm.at[0], w_in_v.at[0]),
                (gate_hbm, gate_v),
                (labels_hbm, labels_v),
                (bias_hbm, bias_v),
                (out_hbm, out_v),
                (out_bias_hbm, out_bias_v),
            )
        )
    ]
    for load in loads:
        load.start()
    pl.semaphore_wait(barrier, n_ex + n_chip)

    steps = [(a, b) for a in range(n_yh) for b in range(n_z) if a or b]
    steps.sort(key=lambda s: -(2 * min(s[0], n_yh - s[0]) + min(s[1], n_z - s[1])))

    def spread(src_of, dst, send, recv):
        for a, b in steps:
            to_ex = lax.rem(y_hi + a, n_yh) * n_z + lax.rem(z + b, n_z)
            remote(src_of(to_ex), dst.at[ex], send, recv, (dp, to_ex)).start()

    def spread_wait(dst, send, recv):
        every = dst.at[pl.ds(0, n_ex - 1)]
        copy = remote(every, every, send, recv, ex_peer(1))
        copy.wait_recv()
        copy.wait_send()

    def unshuffle(src, dst, count):
        rows = src.shape[1]
        shuf[pl.ds(0, n_ex * rows), :] = src[...].astype(F32).reshape(n_ex * rows, LANES)
        for j in range(count):
            for i in range(2):
                piece = shuf[pl.ds(j * 2 + i, n_ex, stride=rows), :]
                dst[i * n_ex : (i + 1) * n_ex, j * LANES : (j + 1) * LANES] = piece.astype(BF)

    own_load.wait()
    spread(lambda _: first_buf.at[ex], first_buf, first_send, first_recv)
    w_in_copy = remote(w_in_hbm.at[0], w_in_v.at[1], w_send.at[0], w_recv.at[0], sibling)
    w_in_copy.start()
    for load in loads[4:8]:
        load.wait()
    for t in range(tasks):
        for j in range(width // LANES):
            at = (t * (width // LANES) + j) * 2
            cols = slice(j * LANES, (j + 1) * LANES)
            for i in range(2):
                small[0, at + i : at + i + 1, :] = bias_v[t : t + 1, cols]
                small[1, at + i : at + i + 1, :] = out_v[t : t + 1, cols]
            label = labels_v[:, t : t + 1].astype(F32)
            small[2, at : at + 2, :] = jnp.broadcast_to(label, (2, LANES))
            small[3, at : at + 2, :] = jnp.broadcast_to(out_bias_v[:, t : t + 1], (2, LANES))
    loads[0].wait()
    loads[1].wait()
    for t in range(tasks):
        cols = slice(t * width, (t + 1) * width)
        fused[0, :, cols] = dot(w_out_v[...], tower_v[t]).astype(BF)
    fused_copy = remote(fused.at[0], fused.at[1], w_send.at[1], w_recv.at[1], sibling)
    fused_copy.start()
    loads[3].wait()
    same_task = ones_where((gates, gates), lambda r, c: r // experts == c // experts)
    own_share = ones_where(
        (gates, wide), lambda r, c: (r // experts == c // width) & (r % experts == ex)
    )

    def gate_probs(rows):
        logits = dot_nt(rows, gate_v[...])
        lane = lax.broadcasted_iota(jnp.int32, logits.shape, 1) // experts
        top = jnp.zeros_like(logits)
        for t in range(tasks):
            mine = lane == t
            peak = jnp.max(jnp.where(mine, logits, -jnp.inf), axis=1, keepdims=True)
            top = jnp.where(mine, peak, top)
        grown = jnp.exp(logits - top)
        high, low = split(grown)
        return grown / (dot(high, same_task) + dot(low, same_task))

    def shares(probs):
        high, low = split(probs)
        return dot(high, own_share) + dot(low, own_share)

    spread_wait(first_buf, first_send, first_recv)
    unshuffle(first_buf, ev_a.at[chip], feat // LANES)

    def to_chips(buf, send, recv):
        @pl.loop(1, n_chip)
        def _(k):
            mine = buf.at[chip]
            remote(mine, buf.at[chip], send.at[k], recv.at[chip], chip_peer(k)).start()

    def arrived(buf, send, recv, slot):
        remote(buf.at[slot], buf.at[slot], send.at[0], recv.at[slot], sibling).wait_recv()

    def forward(buf, other, send, recv, slot):
        remote(buf.at[slot], other.at[slot], send.at[slot], recv.at[slot], sibling).start()

    def sends_done(buf, send, first, last):
        @pl.loop(first, last)
        def _(k):
            remote(buf.at[0], buf.at[0], send.at[k], send.at[k], sibling).wait_send()

    left = y_lo * n_x + lax.rem(x + n_x - 1, n_x)
    right = y_lo * n_x + lax.rem(x + 1, n_x)
    across = y_lo * n_x + lax.rem(x + 2, n_x)
    other_row = (1 - 2 * y_lo) * n_x

    class Gather:
        def __init__(self, parts, buf, twin, send, recv, twin_send, twin_recv):
            self.buf, self.twin, self.send, self.recv = buf, twin, send, recv
            self.twin_send, self.twin_recv = twin_send, twin_recv
            self.rows = blk // parts
            self.up = list(range(parts // 2))
            self.down = list(range(parts // 2, parts))
            self.count = 0

        def part(self, slot, p):
            return self.buf.at[slot, pl.ds(p * self.rows, self.rows)]

        def push(self, slot, p, to):
            ref = self.part(slot, p)
            remote(ref, ref, self.send.at[self.count], self.recv.at[slot, p], to).start()
            self.count += 1

        def got(self, slot, p):
            ref = self.part(slot, p)
            remote(ref, ref, self.send.at[0], self.recv.at[slot, p], sibling).wait_recv()

        def pass_on(self, slot):
            remote(
                self.buf.at[slot],
                self.twin.at[slot],
                self.twin_send.at[slot],
                self.twin_recv.at[slot],
                sibling,
            ).start()

        def begin(self):
            for u, d in zip(self.up, self.down):
                self.push(chip, u, x_peer(1))
                self.push(chip, d, x_peer(-1))
                self.push(chip, u, y_peer(1))
                self.push(chip, d, y_peer(-1))
            for u, d in zip(self.up, self.down):
                self.push(chip, d, x_peer(1))
                self.push(chip, u, x_peer(-1))
            self.pass_on(chip)

        def sides(self):
            for u, d in zip(self.up, self.down):
                self.got(left, u)
                self.push(left, u, x_peer(1))
                self.push(left, u, y_peer(1))
                self.got(right, d)
                self.push(right, d, x_peer(-1))
                self.push(right, d, y_peer(-1))
            for u, d in zip(self.up, self.down):
                self.got(left, d)
                self.push(left, d, y_peer(-1))
                self.got(right, u)
                self.push(right, u, y_peer(1))
            self.pass_on(left)
            self.pass_on(right)

        def opposite(self):
            for u, d in zip(self.up, self.down):
                self.got(across, u)
                self.push(across, u, y_peer(1))
                self.got(across, d)
                self.push(across, d, y_peer(-1))
            self.pass_on(across)

        def other(self, slot):
            slot = slot + other_row
            for p in self.up + self.down:
                self.got(slot, p)
            self.pass_on(slot)
            return slot

        def twin_row(self, first):
            @pl.loop(0, n_x)
            def _(k):
                arrived(self.twin, self.send, self.twin_recv, first + k)

        def sent(self):
            ref = self.part(0, 0)

            @pl.loop(0, self.count)
            def _(k):
                remote(ref, ref, self.send.at[k], self.recv.at[0, 0], sibling).wait_send()

            sends_done(self.buf, self.twin_send, 0, n_chip)

    events = Gather(EV_PARTS, ev_a, ev_b, ev_send, ev_recv, evf_send, evf_recv)
    events.begin()
    probs = gate_probs(ev_a[chip])
    prob_own[...] = probs
    share_own[...] = shares(probs)
    loads[2].wait()
    w_in_copy.wait_recv()
    fused_copy.wait_recv()

    def forward_block(slot):
        rows = ev_a[slot]
        part = None
        for h in range(2):
            pre = dot(rows, w_in_v[h])
            hidden = gelu_parts(pre)[0].astype(BF)
            term = dot(hidden, fused[h])
            part = term if part is None else part + term
        return part

    def send_part(slot, sem):
        part_send[slot] = forward_block(slot).astype(BF)
        to = (slot * CORES + core, ex)
        remote(
            part_send.at[slot], part_recv.at[chip], part_ssem.at[sem], part_rsem.at[chip], to
        ).start()

    part_own[...] = forward_block(chip)
    send_part(events.other(chip), 4)
    events.sides()
    send_part(left, 1)
    send_part(right, 2)
    events.opposite()
    send_part(across, 3)
    send_part(events.other(left), 5)
    send_part(events.other(right), 6)
    send_part(events.other(across), 7)

    def prepare(group, buf, at):
        rows = buf[pl.ds(at * per_group, per_group)].reshape(g_rows, feat)
        pre = dot(rows, w_in_v[0])
        value, slope = gelu_parts(pre)
        slope_v[group] = slope
        hidden_t[group] = value.T.astype(BF)
        ev_t[group] = rows.astype(F32).T.astype(BF)
        share[group] = shares(gate_probs(rows))

    @pl.loop(0, half)
    def _(g):
        prepare(g, ev_a, g)

    events.twin_row(0)
    events.twin_row(n_x)

    @pl.loop(0, half)
    def _(g):
        prepare(half + g, ev_b, g)

    total = part_own[...]
    for k in range(1, n_chip):
        slot = lax.rem(chip + k, n_chip)
        arrived(part_recv, part_ssem, part_rsem, slot)
        total = total + part_recv[slot].astype(F32)
    terms = total * share_own[...]
    crow = term_send.shape[1]
    for j in range(wide // LANES):
        for i in range(2):
            shuf[pl.ds(j * 2 + i, n_ex, stride=crow), :] = terms[
                i * n_ex : (i + 1) * n_ex, j * LANES : (j + 1) * LANES
            ]
    term_send[...] = shuf[pl.ds(0, n_ex * crow), :].reshape(n_ex, crow, LANES).astype(BF)
    spread(lambda to: term_send.at[to], term_recv, term_ssem, term_rsem)
    term_recv[ex] = term_send[ex]
    spread_wait(term_recv, term_ssem, term_rsem)

    def both_halves(value):
        row = lax.broadcasted_iota(jnp.int32, value.shape, 0)
        step = 2
        while step < 2 * (width // LANES):
            up = pltpu.roll(value, crow - step, 0)
            down = pltpu.roll(value, step, 0)
            value = value + jnp.where((row // step) % 2 == 0, up, down)
            step *= 2
        return value

    mixed = jnp.sum(term_recv[...].astype(F32), axis=0)
    act, act_slope = gelu_parts(mixed + small[0])
    weight = small[1]
    summed = jnp.broadcast_to(jnp.sum(act * weight, axis=1, keepdims=True), mixed.shape)
    logit = both_halves(summed) + small[3]
    dlogit = 1.0 / (1.0 + jnp.exp(-logit)) - small[2]
    dt = (dlogit * weight * act_slope).astype(BF)
    dt_chunk[...] = dt
    spread(lambda _: dt_chunk, dt_first, dt1_send, dt1_recv)
    dt_first[ex] = dt

    prod = (term_recv[...].astype(F32) * dt.astype(F32)[None]).reshape(n_ex * crow, LANES)
    high, low = split(prod)
    all_ones = jnp.ones((LANES, gates), BF)
    sums = dot(high, all_ones) + dot(low, all_ones)
    at = lax.broadcasted_iota(jnp.int32, sums.shape, 0)
    lane = lax.broadcasted_iota(jnp.int32, sums.shape, 1)
    here = lane == (at % crow) // (2 * (width // LANES)) * experts + at // crow
    sums = jnp.where(here, sums, 0.0)
    pick = ones_where((16, n_ex * crow), lambda r, c: (r == c % 2))
    high, low = split(sums)
    moved = dot(pick, high) + dot(pick, low)
    high, low = split(moved)
    weighted = dot(high, same_task) + dot(low, same_task)
    own_rows = jnp.concatenate(
        [
            prob_own[pl.ds(ex, 1), :],
            prob_own[pl.ds(n_ex + ex, 1), :],
            jnp.zeros((14, gates), F32),
        ],
        axis=0,
    )
    dg = (moved - own_rows * weighted).astype(BF)
    dg_chunk[...] = dg
    spread(lambda _: dg_chunk, dg_first, dg1_send, dg1_recv)
    dg_first[ex] = dg

    w_in_copy.wait_send()
    fused_copy.wait_send()
    events.sent()
    sends_done(part_send, part_ssem, 1, n_chip)

    spread_wait(dt_first, dt1_send, dt1_recv)
    unshuffle(dt_first, dt_a.at[chip], wide // LANES)
    towers = Gather(DT_PARTS, dt_a, dt_b, dt_send, dt_recv, dtf_send, dtf_recv)
    towers.begin()
    spread_wait(dg_first, dg1_send, dg1_recv)
    rows16 = dg_first.shape[1]
    shuf2 = shuf.at[pl.ds(0, n_ex * rows16)]
    shuf2[:, 0:gates] = dg_first[...].astype(F32).reshape(n_ex * rows16, gates)
    for i in range(2):
        dg_a[chip, i * n_ex : (i + 1) * n_ex, :] = shuf2[pl.ds(i, n_ex, stride=rows16), :][
            :, 0:gates
        ].astype(BF)
    to_chips(dg_a, dg_send, dg_recv)
    forward(dg_a, dg_b, dgf_send, dgf_recv, chip)

    acc_in[...] = jnp.zeros_like(acc_in)
    acc_mid[...] = jnp.zeros_like(acc_mid)
    acc_gate[...] = jnp.zeros_like(acc_gate)

    def backward(group, dt_buf, at):
        span = pl.ds(at * per_group, per_group)
        dout = (dt_buf[span].reshape(g_rows, wide).astype(F32) * share[group]).astype(BF)
        dhidden = dot_nt(dout, fused[0])
        dpre = (dhidden * slope_v[group]).astype(BF)
        acc_in[...] += dot(ev_t[group], dpre)
        acc_mid[...] += dot(hidden_t[group], dout)

    def gate_rows(ev_buf, dg_buf, at):
        span = pl.ds(at * per_group, per_group)
        rows = ev_buf[span].reshape(g_rows, feat)
        acc_gate[...] += dot(dg_buf[span].reshape(g_rows, gates).astype(F32).T.astype(BF), rows)

    towers.sides()

    @pl.loop(1, n_chip)
    def _(k):
        slot = lax.rem(chip + k, n_chip)
        arrived(dg_a, dg_send, dg_recv, slot)
        forward(dg_a, dg_b, dgf_send, dgf_recv, slot)

    for g in range(half):
        gate_rows(ev_a, dg_a, g)
    towers.opposite()
    backward(y_lo, dt_a, y_lo)
    towers.other(chip)
    towers.other(left)
    towers.other(right)
    towers.twin_row(y_lo * n_x)
    backward(half + y_lo, dt_b, y_lo)

    @pl.loop(0, n_chip)
    def _(k):
        arrived(dg_b, dgf_send, dgf_recv, k)

    for g in range(half):
        gate_rows(ev_b, dg_b, g)
    towers.other(across)
    backward(1 - y_lo, dt_a, 1 - y_lo)
    mine = ones_where((16, gates), lambda r, c: (c == r * experts + ex))
    high, low = split(acc_gate[...])
    gate_sums = dot(mine, high) + dot(mine, low)
    for t in range(tasks):
        grad_gate_ref[t] = gate_sums[t : t + 1]
    sends_done(dg_a, dg_send, 1, n_chip)
    sends_done(dg_a, dgf_send, 0, n_chip)
    towers.sent()
    towers.twin_row((1 - y_lo) * n_x)
    backward(half + 1 - y_lo, dt_b, 1 - y_lo)

    grad_in_ref[...] = acc_in[...].astype(BF)
    mid = acc_mid[...].astype(BF)
    result = None
    for t in range(tasks):
        term = dot_nt(mid[:, t * width : (t + 1) * width], tower_v[t])
        result = term if result is None else result + term
    grad_out_ref[...] = result.astype(BF)


def per_device(
    n_dp,
    n_ex,
    events,
    labels,
    w_in,
    w_out,
    gate_weight,
    tower_in,
    tower_bias,
    tower_out,
    tower_out_bias,
):
    tasks, feat, width = tower_in.shape
    experts = gate_weight.shape[2]
    hid = w_out.shape[1]
    n_chip = n_dp // CORES
    own = events.shape[0]
    blk = own * n_ex
    plane = n_chip * blk
    g_rows = max(plane // 2, blk)
    groups = 2 * plane // g_rows
    wide = tasks * width
    gates = tasks * experts
    chunk = own * feat // LANES
    chunk_t = own * wide // LANES
    chunk_events = events.reshape(own, feat // LANES, LANES).transpose(1, 0, 2).reshape(chunk, LANES)
    vmem = pl.BlockSpec(memory_space=pltpu.VMEM)
    hbm = pl.BlockSpec(memory_space=pltpu.HBM)
    dma = pltpu.SemaphoreType.DMA
    scratch = [
        pltpu.VMEM((n_ex, chunk, LANES), BF),
        pltpu.VMEM((n_ex * max(chunk, chunk_t, 16), LANES), F32),
        pltpu.VMEM((n_chip, blk, feat), BF),
        pltpu.VMEM((n_chip, blk, feat), BF),
        pltpu.VMEM((2, feat, hid), BF),
        pltpu.VMEM((hid, feat), BF),
        pltpu.VMEM((2, hid, wide), BF),
        pltpu.VMEM((tasks, feat, width), BF),
        pltpu.VMEM((gates, feat), BF),
        pltpu.VMEM((own, tasks), jnp.int32),
        pltpu.VMEM((tasks, width), F32),
        pltpu.VMEM((tasks, width), F32),
        pltpu.VMEM((1, tasks), F32),
        pltpu.VMEM((blk, wide), F32),
        pltpu.VMEM((n_chip, blk, wide), BF),
        pltpu.VMEM((n_chip, blk, wide), BF),
        pltpu.VMEM((n_ex, chunk_t, LANES), BF),
        pltpu.VMEM((n_ex, chunk_t, LANES), BF),
        pltpu.VMEM((4, chunk_t, LANES), F32),
        pltpu.VMEM((blk, gates), F32),
        pltpu.VMEM((blk, wide), F32),
        pltpu.VMEM((groups, g_rows, wide), F32),
        pltpu.VMEM((groups, g_rows, hid), F32),
        pltpu.VMEM((groups, hid, g_rows), BF),
        pltpu.VMEM((groups, feat, g_rows), BF),
        pltpu.VMEM((chunk_t, LANES), BF),
        pltpu.VMEM((n_ex, chunk_t, LANES), BF),
        pltpu.VMEM((n_chip, blk, wide), BF),
        pltpu.VMEM((n_chip, blk, wide), BF),
        pltpu.VMEM((16, gates), BF),
        pltpu.VMEM((n_ex, 16, gates), BF),
        pltpu.VMEM((n_chip, blk, gates), BF),
        pltpu.VMEM((n_chip, blk, gates), BF),
        pltpu.VMEM((feat, hid), F32),
        pltpu.VMEM((hid, wide), F32),
        pltpu.VMEM((gates, feat), F32),
        dma((9,)),
        dma((2,)),
        dma((2,)),
        dma,
        dma,
        dma((7 * EV_PARTS,)),
        dma((n_chip, EV_PARTS)),
        dma((n_chip,)),
        dma((n_chip,)),
        dma((n_chip,)),
        dma((n_chip,)),
        dma,
        dma,
        dma,
        dma,
        dma,
        dma,
        dma((7 * DT_PARTS,)),
        dma((n_chip, DT_PARTS)),
        dma((n_chip,)),
        dma((n_chip,)),
        dma((n_chip,)),
        dma((n_chip,)),
        dma((n_chip,)),
        dma((n_chip,)),
    ]
    grad_in, grad_out, grad_gate = pl.pallas_call(
        functools.partial(kernel, n_ex, n_chip, tasks, width),
        out_shape=(
            jax.ShapeDtypeStruct((feat, hid), BF),
            jax.ShapeDtypeStruct((hid, feat), BF),
            jax.ShapeDtypeStruct((tasks, 1, feat), F32),
        ),
        in_specs=[hbm] * 9,
        out_specs=(vmem, vmem, vmem),
        scratch_shapes=scratch,
        compiler_params=pltpu.CompilerParams(
            collective_id=0, has_side_effects=True, vmem_limit_bytes=VMEM_MIB * 1024 * 1024
        ),
    )(
        *(
            pltpu.with_memory_space_constraint(operand, pltpu.HBM)
            for operand in (
                chunk_events,
                labels,
                w_in,
                w_out,
                gate_weight.transpose(0, 2, 1).reshape(gates, feat),
                tower_in,
                tower_bias,
                tower_out,
                tower_out_bias.reshape(1, tasks),
            )
        )
    )
    return grad_in[None], grad_out[None], grad_gate.transpose(0, 2, 1)


def solution(mesh):
    placed = (
        P(("dp", "expert"), None),
        P(("dp", "expert"), None),
        P("expert", None, "dp"),
        P("expert", "dp", None),
        P(),
        P(),
        P(),
        P(),
        P(),
    )
    return jax.shard_map(
        functools.partial(per_device, mesh.shape["dp"], mesh.shape["expert"]),
        mesh=mesh,
        in_specs=placed,
        out_specs=(P("expert", None, "dp"), P("expert", "dp", None), P(None, None, "expert")),
        check_vma=False,
    )
```
